512 devices in a mesh: tensor: 4 (over y), shard: 32 (over x_hi, z), replica: 4 (over x_lo, core).
Axes of the slice: x: 4 (x_hi: 2, x_lo: 2; x = x_hi * 2 + x_lo), y: 4, z: 16, core: 2. Of those that a mesh axis runs over, the one named last changes fastest.
Arguments:
- activations: bfloat16 [32768, 8192], P(('shard', 'replica'), 'tensor'), may hold values from -6 to 6
- queries: bfloat16 [32768, 4096], P(('shard', 'replica'), 'tensor'), may hold values from -48 to 48
- key_vectors: bfloat16 [32768, 512], P(('shard', 'replica'), 'tensor'), may hold values from -4 to 4
- grad_output: bfloat16 [32768, 4096], P(('shard', 'replica'), 'tensor'), may hold values from -6 to 6
- segment_ids: int32 [32768], P(('shard', 'replica')), may hold values from 0 to 511, never falling along the last dimension, each value on 1 to 128 neighbouring positions
- value_weight: bfloat16 [8192, 512], P('shard', 'tensor'), may hold values from -0.0625 to 0.0625
- master: float32 [8192, 512], P('shard', 'tensor'), may hold values from -3 to 3
- first_moment: float32 [8192, 512], P('shard', 'tensor'), may hold values from -3 to 3
- second_moment: float32 [8192, 512], P('shard', 'tensor'), may hold values from 0.01 to 1
Outputs:
- grad_queries: bfloat16 [32768, 4096], P(('shard', 'replica'), 'tensor')
- grad_keys: bfloat16 [32768, 512], P(('shard', 'replica'), 'tensor')
- gradient: float32 [8192, 512], P('shard', 'tensor')
- new_master: float32 [8192, 512], P('shard', 'tensor')
- new_first: float32 [8192, 512], P('shard', 'tensor')
- new_second: float32 [8192, 512], P('shard', 'tensor')
The draws below stay inside these ranges and needn't reach their ends.
Inputs may be any that keep to these rules, and one draw needn't show every extreme that they name: `segment_ids`: never falls along the tokens; each document spans at most half of 256 positions, and one spans exactly that many.
All inputs are finite; a program needn't handle non-finite values.
Results may differ from the reference program's by a relative error of at most 0.025.
Values may be sent and summed in bfloat16 or wider, within the bound.
A program may use at most 64 MiB of HBM per device.

```python
import math
import jax
import jax.numpy as jnp
import numpy as np
from jax import lax

D = 8192
HD = 128
GROUP = 8
TOK_DEV = 256
STEP = 10
KV_HEADS = 4
Q_HEADS = 32
TOKENS = 32768
N_SHARD = 32
N_REPLICA = 4


def key_table(key):
    shape = (TOKENS, KV_HEADS, HD)
    normal_part = jnp.clip(jax.random.normal(key, shape, jnp.float32), -4.0, 4.0)
    base = normal_part
    chosen = (jnp.arange(TOKENS) % 29 == 2)[:, None, None]
    return jnp.where(chosen, base, base)


def draw_key_vectors(key, part):
    table = key_table(key)
    return table.reshape(TOKENS, KV_HEADS * HD).astype(jnp.bfloat16)


def draw_queries(key, part):
    shape = (TOKENS, KV_HEADS, GROUP, HD)
    key = jax.random.fold_in(key, 11)
    result = jnp.clip(jax.random.normal(key, shape, jnp.float32), -4.0, 4.0)
    return result.reshape(TOKENS, KV_HEADS * GROUP * HD).astype(jnp.bfloat16)


def levels(rng, dims, shards, low, largest):
    loudness = 1.0
    for dim, parts in shards:
        steps = jax.random.uniform(jax.random.fold_in(jax.random.fold_in(rng, 6), dim), (parts,), jnp.float32, low / len(shards), largest / len(shards))
        loudness = loudness * jnp.repeat(jnp.exp(steps), dims[dim] // parts).reshape((-1,) + (1,) * (len(dims) - 1 - dim))
    return loudness


def split_up(count, total, most, lean):
    weights = [(1 << 20) // math.isqrt(grade ** lean) + 1 for grade in range(2, count + 1)]
    spare, given = total - most - (count - 1), [1] * (count - 1)
    while spare > 0:
        movable = [i for i in range(count - 1) if given[i] < most]
        whole, remaining = sum([weights[i] for i in movable]), spare
        for i in movable:
            extra = min(most - given[i], max(1, remaining * weights[i] // whole), spare)
            given[i] = given[i] + extra
            spare = spare - extra
    return np.array([most] + given)


def uneven(key, number_of, total, reach, lean):
    if number_of == 2:
        one = jax.random.randint(key, (), max(1, total - reach), min(reach, total - 1) + 1)
        return jnp.stack([one, total - one])
    tallies = jnp.asarray(split_up(number_of, total, reach, lean), jnp.int32)
    couples = (number_of - 1) // 2
    source_of, receiver = tallies[1:1 + 2 * couples:2], tallies[2:2 + 2 * couples:2]
    slack = jnp.minimum(source_of - 1, reach - receiver)
    passed = jax.random.randint(jax.random.fold_in(key, 1), (couples,), 0, 1 << 20) % (slack + 1)
    tallies = tallies.at[1:1 + 2 * couples:2].set(source_of - passed).at[2:2 + 2 * couples:2].set(receiver + passed)
    return tallies[jax.random.permutation(jax.random.fold_in(key, 2), number_of)]


def scatter_about(key, extent, width, most, shards=(), held_as=jnp.bfloat16):
    factor_of = levels(key, extent, shards, -0.22, 0.18) if shards else 1.0
    drawn = jax.random.normal(key, extent, jnp.float32) * width * factor_of
    return jnp.minimum(jnp.maximum(drawn, -most), most).astype(held_as)


def setup_inputs(seed: int = 0) -> dict:
    key_of = jax.random.split(jax.random.key(seed), 10)
    activations = scatter_about(key_of[0], (TOKENS, D), 1.0, 6.0, ((0, 128), (1, 4)))
    queries = draw_queries(jax.random.fold_in(key_of[9], 71), 0)
    key_vectors = draw_key_vectors(jax.random.fold_in(key_of[9], 71), 0)
    grad_output = scatter_about(key_of[3], (TOKENS, Q_HEADS * HD), 1.0, 6.0, ((0, 128), (1, 4)))
    segment_ids = jnp.searchsorted(jnp.cumsum(uneven(key_of[4], 4 * N_SHARD * N_REPLICA, TOKENS, TOK_DEV // 2, 1)), jnp.arange(TOKENS), side="right").astype(jnp.int32)
    value_weight = scatter_about(key_of[5], (D, KV_HEADS * HD), D ** -0.5, 0.0625, ((0, 32), (1, 4)))
    master = scatter_about(key_of[6], (D, KV_HEADS * HD), 0.5, 3.0, ((0, 32), (1, 4)), jnp.float32)
    first_moment = scatter_about(key_of[7], (D, KV_HEADS * HD), 0.5, 3.0, ((0, 32), (1, 4)), jnp.float32)
    second_moment = jnp.clip(jnp.exp(math.log(1.0) - 4.6051702 * jax.random.uniform(key_of[8], (D, KV_HEADS * HD), jnp.float32) ** levels(key_of[8], (D, KV_HEADS * HD), ((0, 32), (1, 4)), -0.2, 0.2)), 0.01, 1.0)
    return {"activations": activations, "queries": queries, "key_vectors": key_vectors, "grad_output": grad_output, "segment_ids": segment_ids, "value_weight": value_weight, "master": master, "first_moment": first_moment, "second_moment": second_moment}


BETA_FIRST = 0.9
BETA_SECOND = 0.95
LEARN_RATE = 0.001
WEIGHT_DECAY = 0.1
EPSILON = 1e-08

def block_grads(query_block, key_rows, values, grad_block, seg_block, all_segments, pos_block, positions, factor):
    query_wide = query_block.astype(jnp.float32)
    key_wide = key_rows.astype(jnp.float32)
    value_wide = values.astype(jnp.float32)
    grad_wide = grad_block.astype(jnp.float32)
    scores = jnp.einsum('bgd,td->gbt', query_wide, key_wide) * factor
    allowed = (seg_block[:, None] == all_segments[None, :]) & (positions[None, :] <= pos_block[:, None])
    scores = jnp.where(allowed[None], scores, -1e+30)
    row_max = lax.optimization_barrier(jnp.max(scores, axis=2, keepdims=True))
    powered = jnp.exp(scores - row_max)
    weights = powered / lax.optimization_barrier(jnp.sum(powered, axis=2, keepdims=True))
    rounded = weights.astype(jnp.bfloat16)
    rounded_wide = rounded.astype(jnp.float32)
    outputs = jnp.einsum('gbt,td->bgd', rounded_wide, value_wide)
    row_dot = lax.optimization_barrier(jnp.sum(grad_wide * outputs, axis=2))
    grad_weights = jnp.einsum('bgd,td->gbt', grad_wide, value_wide)
    grad_scores = (weights * (grad_weights - jnp.transpose(row_dot)[:, :, None]) * factor).astype(jnp.bfloat16)
    score_wide = grad_scores.astype(jnp.float32)
    query_grad = jnp.einsum('gbt,td->bgd', score_wide, key_wide).astype(jnp.bfloat16)
    key_grad = jnp.einsum('gbt,bgd->td', score_wide, query_wide)
    value_grad = jnp.einsum('gbt,bgd->td', rounded_wide, grad_wide)
    return (query_grad, key_grad, value_grad)

def reference(activations, queries, key_vectors, grad_output, segment_ids, value_weight, master, first_moment, second_moment):
    rank_count = N_SHARD * N_REPLICA
    factor = 1.0 / math.sqrt(HD)
    positions = jnp.arange(TOK_DEV, dtype=jnp.int32)

    def one_rank(carry, number):
        lower = (number * TOK_DEV).astype(jnp.int32)
        rows_input = lax.dynamic_slice_in_dim(activations, lower, TOK_DEV, 0)
        rows_query = lax.dynamic_slice_in_dim(queries, lower, TOK_DEV, 0)
        rows_key = lax.dynamic_slice_in_dim(key_vectors, lower, TOK_DEV, 0)
        rows_grad = lax.dynamic_slice_in_dim(grad_output, lower, TOK_DEV, 0)
        rows_segment = lax.dynamic_slice_in_dim(segment_ids, lower, TOK_DEV, 0)
        values_all = jnp.dot(rows_input, value_weight, preferred_element_type=jnp.float32).astype(jnp.bfloat16)
        query_parts = []
        key_parts = []
        value_parts = []
        for kv_index in range(KV_HEADS):
            span = GROUP * HD
            query_heads = rows_query[:, kv_index * span:(kv_index + 1) * span].reshape(TOK_DEV, GROUP, HD)
            grad_heads = rows_grad[:, kv_index * span:(kv_index + 1) * span].reshape(TOK_DEV, GROUP, HD)
            key_head = rows_key[:, kv_index * HD:(kv_index + 1) * HD]
            value_head = values_all[:, kv_index * HD:(kv_index + 1) * HD]
            query_grad, key_grad, value_grad = block_grads(query_heads, key_head, value_head, grad_heads, rows_segment, rows_segment, positions, positions, factor)
            query_parts.append(query_grad.reshape(TOK_DEV, span))
            key_parts.append(key_grad.astype(jnp.bfloat16))
            value_parts.append(value_grad.astype(jnp.bfloat16))
        value_low = jnp.concatenate(value_parts, axis=1)
        term = jnp.dot(jnp.transpose(rows_input), value_low, preferred_element_type=jnp.float32)
        term = term.astype(jnp.bfloat16).astype(jnp.float32)
        return (carry + term, (jnp.concatenate(query_parts, axis=1), jnp.concatenate(key_parts, axis=1)))
    zeroed = jnp.zeros((D, KV_HEADS * HD), jnp.float32)
    summed, (query_all, key_all) = lax.scan(one_rank, zeroed, jnp.arange(rank_count, dtype=jnp.int32))
    grad_queries = query_all.reshape(TOKENS, Q_HEADS * HD)
    grad_keys = key_all.reshape(TOKENS, KV_HEADS * HD)
    gradient = summed / rank_count
    new_first = BETA_FIRST * first_moment + (1.0 - BETA_FIRST) * gradient
    new_second = BETA_SECOND * second_moment + (1.0 - BETA_SECOND) * gradient * gradient
    corrected = new_first / (1.0 - BETA_FIRST ** STEP) / (jnp.sqrt(new_second / (1.0 - BETA_SECOND ** STEP)) + EPSILON)
    new_master = master - LEARN_RATE * (corrected + WEIGHT_DECAY * master)
    return (grad_queries, grad_keys, gradient, new_master, new_first, new_second)
```

```python
import functools
import math

import jax
import jax.numpy as jnp
from jax import lax
from jax.experimental import pallas as pl
from jax.experimental.pallas import tpu as pltpu
from jax.sharding import PartitionSpec as P

STEP = 10
BETA_FIRST = 0.9
BETA_SECOND = 0.95
LEARN_RATE = 0.001
WEIGHT_DECAY = 0.1
EPSILON = 1e-08

F32 = jnp.float32
BF16 = jnp.bfloat16
MESH = pl.DeviceIdType.MESH
TOK = 256
HD = 128
HEADS = 8
HALF = 1024
QTR = 256
RANKS = 128
FACTOR = 1.0 / math.sqrt(HD)
NT = (((1,), (1,)), ((), ()))


def place(x, y, z, c):
    return (y, (x // 2) * 16 + z, (x % 2) * 2 + c)


def kernel(
    act, que, key, gout, seg, wgt, mas, fst, snd,
    o_gq, o_gk, o_grad, o_mas, o_fst, o_snd,
    a2, qv, kv, gov, segv, masv, fstv, sndv,
    wbuf, bias, wst, gv, gt, tt, tmg, r1, sx, zr, rb, ob, gf,
    pp, pr, vs, vr, vals, ktr, gk, gqv, gkv, og, om, of, osn,
    ssem, rsem, lsem,
):
    y = lax.axis_index("tensor")
    s = lax.axis_index("shard")
    r = lax.axis_index("replica")
    z = s % 16
    c = r % 2
    x = (s // 16) * 2 + r // 2

    ids = [0]

    def new_id(n=1):
        ids[0] += n
        return ids[0] - n

    def send(src, dst, i, dev):
        cp = pltpu.make_async_remote_copy(
            src_ref=src, dst_ref=dst, send_sem=ssem.at[i], recv_sem=rsem.at[i],
            device_id=dev, device_id_type=MESH,
        )
        cp.start()
        sends.append((src, i))

    def got(ref, i):
        pltpu.make_async_copy(ref, ref, rsem.at[i]).wait()

    sends = []
    xr, xl = (x + 1) % 4, (x + 3) % 4
    xo = (x + 2) % 4
    c_dev = place(x, y, z, 1 - c)
    xr_dev, xl_dev = place(xr, y, z, c), place(xl, y, z, c)

    def y_dev(d):
        return place(x, (y + d) % 4, z, c)

    def z_dev(d):
        return place(x, y, (z + d + 16) % 16, c)

    s_y, s_c, s_x = s // 8, (s % 8) // 4, s % 4
    own_s, own_y = 8 * y + 4 * c + x, z % 4

    def rep_dev(k):
        return place(s_x, s_y, 4 * k + y, s_c)

    def owner_dev(k):
        return (own_y, own_s, k)

    is_self = jnp.logical_and(own_s == s, own_y == y)

    barrier = pltpu.get_barrier_semaphore()
    for dev in [c_dev, xr_dev, xl_dev, place(x + 1 - 2 * (x % 2), y, z, 1 - c)] + [
        y_dev(d) for d in (1, 2, 3)
    ] + [z_dev(d) for d in (-2, -1, 1, 2)]:
        pl.semaphore_signal(barrier, inc=1, device_id=dev, device_id_type=MESH)
    for k in range(4):
        @pl.when(jnp.logical_not(jnp.logical_and(is_self, k == r)))
        def _():
            pl.semaphore_signal(barrier, inc=1, device_id=owner_dev(k), device_id_type=MESH)

        @pl.when(jnp.logical_not(jnp.logical_and(is_self, k == z // 4)))
        def _():
            pl.semaphore_signal(barrier, inc=1, device_id=rep_dev(k), device_id_type=MESH)

    mine = pl.ds(pl.multiple_of(TOK * c, TOK), TOK)
    theirs = pl.ds(pl.multiple_of(TOK * (1 - c), TOK), TOK)
    loads = [
        (que, qv), (key, kv), (seg, segv), (gout, gov),
        (act.at[:, pl.ds(pl.multiple_of(HALF * c, HALF), HALF)], a2.at[mine]),
        (mas, masv), (fst, fstv), (snd, sndv),
    ]
    copies = [pltpu.make_async_copy(a, b, lsem.at[n]) for n, (a, b) in enumerate(loads)]
    for cp in copies:
        cp.start()

    pl.semaphore_wait(barrier, 19 - 2 * is_self.astype(jnp.int32))

    w1a = new_id()
    zy = pl.ds(pl.multiple_of(HD * y, HD), HD)
    send(wgt, wbuf.at[s_x, :, zy], w1a, rep_dev((r + 1) % 4))
    a_id = new_id()
    send(act.at[:, pl.ds(pl.multiple_of(HALF * (1 - c), HALF), HALF)], a2.at[mine], a_id, c_dev)

    for cp in copies[:4]:
        cp.wait()
    seg_row = jnp.broadcast_to(segv[...].astype(F32), (TOK, TOK))
    rows = lax.broadcasted_iota(jnp.int32, (TOK, TOK), 0)
    cols = lax.broadcasted_iota(jnp.int32, (TOK, TOK), 1)
    allowed = jnp.logical_and(seg_row.T == seg_row, rows <= cols)
    bias[...] = jnp.where(allowed, 0.0, -1e30)
    ktr[...] = kv[...].astype(F32).T.astype(BF16)

    def forward_head(h, acc):
        lanes = pl.ds(pl.multiple_of(h * HD, HD), HD)
        scores = lax.dot_general(kv[...], qv[:, lanes], NT, preferred_element_type=F32)
        scores = scores * FACTOR + bias[...]
        powered = jnp.exp(scores - jnp.max(scores, axis=0, keepdims=True))
        weights = powered * (1.0 / jnp.sum(powered, axis=0, keepdims=True))
        wst[h] = weights
        return acc + jnp.dot(weights.astype(BF16), gov[:, lanes], preferred_element_type=F32)

    acc = lax.fori_loop(0, HEADS // 2, forward_head, jnp.zeros((TOK, HD), F32))

    zo = pl.ds(pl.multiple_of(HD * own_y, HD), HD)
    got(wbuf.at[x, :, zo], w1a)
    w1b = new_id(3)
    for n, d in enumerate((-1, 1, 2)):
        send(wbuf.at[x, :, zo], wbuf.at[x, :, zo], w1b + n, z_dev(d))

    acc = lax.fori_loop(HEADS // 2, HEADS, forward_head, acc)
    gyt = pl.ds(pl.multiple_of(HD * y, HD), HD)
    gt[gyt, mine] = acc.T.astype(BF16)

    g_y = new_id(3)
    for d in (2, 1, 3):
        send(gt.at[gyt, mine], gt.at[gyt, mine], g_y + d - 1, y_dev(d))
    g_c = new_id(4)
    send(gt.at[gyt, mine], gt.at[gyt, mine], g_c, c_dev)

    for n, d in enumerate((-1, 1, 2)):
        zn = pl.ds(pl.multiple_of(HD * ((z - d + 16) % 4), HD), HD)
        got(wbuf.at[x, :, zn], w1b + n)
    lo, hi = pl.ds(0, HD), pl.ds(HD, HD)
    w2 = new_id(6)
    send(wbuf.at[x, lo], wbuf.at[x, lo], w2, xr_dev)
    send(wbuf.at[x, hi], wbuf.at[x, hi], w2 + 1, xl_dev)
    send(wbuf.at[x, hi], wbuf.at[x, hi], w2 + 2, xr_dev)
    send(wbuf.at[x, lo], wbuf.at[x, lo], w2 + 3, xl_dev)

    for d in (1, 3, 2):
        rows_d = pl.ds(pl.multiple_of(HD * ((y - d + 4) % 4), HD), HD)
        got(gt.at[rows_d, mine], g_y + d - 1)
        send(gt.at[rows_d, mine], gt.at[rows_d, mine], g_c + d, c_dev)
    for cp in copies[4:5]:
        cp.wait()
    got(a2.at[theirs], a_id)
    for n in range(4):
        rows_d = pl.ds(pl.multiple_of(HD * ((y - n + 4) % 4), HD), HD)
        got(gt.at[rows_d, theirs], g_c + n)

    def term(q, half):
        return jnp.dot(
            gt[pl.ds(2 * HD * half, 2 * HD), :],
            a2[:, pl.ds(pl.multiple_of(QTR * q, QTR), QTR)],
            preferred_element_type=F32,
        )

    top, bot = pl.ds(0, 2 * HD), pl.ds(2 * HD, 2 * HD)
    r1_id = new_id(6)
    tt[0] = term(xo, 0).astype(BF16)
    send(tt.at[0], r1.at[0], r1_id, xr_dev)
    tt[1] = term(xo, 1).astype(BF16)
    send(tt.at[1], r1.at[1], r1_id + 1, xl_dev)
    tt[2] = term(xr, 1).astype(BF16)
    send(tt.at[2], r1.at[2], r1_id + 2, xr_dev)
    tt[3] = term(xl, 0).astype(BF16)
    send(tt.at[3], r1.at[3], r1_id + 3, xl_dev)

    got(wbuf.at[xl, lo], w2)
    send(wbuf.at[xl, lo], wbuf.at[xl, lo], w2 + 4, xr_dev)
    got(wbuf.at[xr, hi], w2 + 1)
    send(wbuf.at[xr, hi], wbuf.at[xr, hi], w2 + 5, xl_dev)

    tmg[0] = term(xr, 0)
    tmg[1] = term(xl, 1)
    got(r1.at[0], r1_id)
    tt[4] = (tmg[0] + r1[0].astype(F32)).astype(BF16)
    send(tt.at[4], r1.at[4], r1_id + 4, xr_dev)
    got(r1.at[1], r1_id + 1)
    tt[5] = (tmg[1] + r1[1].astype(F32)).astype(BF16)
    send(tt.at[5], r1.at[5], r1_id + 5, xl_dev)
    sx[top, :] = term(x, 0)
    sx[bot, :] = term(x, 1)

    def values_of(q, first):
        part = jnp.dot(
            a2[:, pl.ds(pl.multiple_of(QTR * q, QTR), QTR)], wbuf[q], preferred_element_type=F32
        )
        pp[...] = part if first else pp[...] + part

    values_of(x, True)
    got(wbuf.at[xl, hi], w2 + 2)
    values_of(xl, False)
    got(wbuf.at[xr, lo], w2 + 3)
    values_of(xr, False)

    got(r1.at[3], r1_id + 3)
    got(r1.at[2], r1_id + 2)
    got(r1.at[4], r1_id + 4)
    got(r1.at[5], r1_id + 5)
    sx[top, :] = sx[top, :] + (r1[3].astype(F32) + r1[4].astype(F32))
    sx[bot, :] = sx[bot, :] + (r1[2].astype(F32) + r1[5].astype(F32))
    z_id = new_id(3)
    for n, d in enumerate((-2, -1, 1)):
        part = pl.ds(pl.multiple_of(HD * ((z + d + 16) % 4), HD), HD)
        zr[3 + n] = sx[part, :].astype(BF16)
        send(zr.at[3 + n], zr.at[n], z_id + n, z_dev(d))

    got(wbuf.at[xo, lo], w2 + 4)
    got(wbuf.at[xo, hi], w2 + 5)
    values_of(xo, False)
    v1 = new_id()
    send(pp.at[theirs], pr, v1, c_dev)

    for n in range(3):
        got(zr.at[n], z_id + n)
    part = pl.ds(pl.multiple_of(HD * own_y, HD), HD)
    rb[...] = (
        sx[part, :] + zr[0].astype(F32) + zr[1].astype(F32) + zr[2].astype(F32)
    ).astype(BF16)
    o_id = new_id(4)
    for k in range(4):
        src = rb.at[pl.ds(32 * k, 32)]
        stay = jnp.logical_and(is_self, k == r)

        @pl.when(jnp.logical_not(stay))
        def _():
            pltpu.make_async_remote_copy(
                src_ref=src, dst_ref=ob.at[z // 4], send_sem=ssem.at[o_id + k],
                recv_sem=rsem.at[o_id + z // 4], device_id=owner_dev(k), device_id_type=MESH,
            ).start()

        @pl.when(stay)
        def _():
            pltpu.make_async_copy(src, ob.at[z // 4], rsem.at[o_id + z // 4]).start()

    got(pr, v1)
    both = pp[mine, :] + pr[...]
    vs[...] = both.astype(BF16)
    pp[mine, :] = both
    v2 = new_id(3)
    for d in (2, 1, 3):
        lanes = pl.ds(pl.multiple_of(HD * ((y + d) % 4), HD), HD)
        send(vs.at[:, lanes], vr.at[d - 1], v2 + d - 1, y_dev(d))

    for k in range(4):
        got(ob.at[k], o_id + k)
    quarter = pl.ds(pl.multiple_of(32 * r, 32), 32)
    gf[quarter, :] = (
        ob[0].astype(F32) + ob[1].astype(F32) + ob[2].astype(F32) + ob[3].astype(F32)
    ) * (1.0 / RANKS)
    f_id = new_id(3)
    for d in (1, 2, 3):
        rd = (r + d) % 4
        send(gf.at[quarter], gf.at[quarter], f_id + d - 1, (y, s, rd))

    for d in (1, 2, 3):
        got(vr.at[d - 1], v2 + d - 1)
    vals[...] = (
        pp[mine, zy] + vr[0].astype(F32) + vr[1].astype(F32) + vr[2].astype(F32)
    ).astype(BF16)

    def backward_head(h, acc):
        lanes = pl.ds(pl.multiple_of(h * HD, HD), HD)
        gw = lax.dot_general(vals[...], gov[:, lanes], NT, preferred_element_type=F32)
        weights = wst[h]
        dots = jnp.sum(weights.astype(BF16).astype(F32) * gw, axis=0, keepdims=True)
        gs = (weights * (gw - dots) * FACTOR).astype(BF16)
        gq = jnp.dot(ktr[...], gs, preferred_element_type=F32)
        gqv[:, lanes] = gq.T.astype(BF16)
        return acc + jnp.dot(gs, qv[:, lanes], preferred_element_type=F32)

    gkv[...] = lax.fori_loop(0, HEADS, backward_head, jnp.zeros((TOK, HD), F32)).astype(BF16)
    outs = [pltpu.make_async_copy(gqv, o_gq, lsem.at[8]), pltpu.make_async_copy(gkv, o_gk, lsem.at[9])]
    for cp in outs:
        cp.start()

    for d in (1, 2, 3):
        other = pl.ds(pl.multiple_of(32 * ((r - d + 4) % 4), 32), 32)
        got(gf.at[other], f_id + d - 1)
    for cp in copies[5:]:
        cp.wait()
    gradient = gf[...].T
    new_first = BETA_FIRST * fstv[...] + (1.0 - BETA_FIRST) * gradient
    new_second = BETA_SECOND * sndv[...] + (1.0 - BETA_SECOND) * gradient * gradient
    corrected = (
        new_first
        / (1.0 - BETA_FIRST**STEP)
        / (jnp.sqrt(new_second / (1.0 - BETA_SECOND**STEP)) + EPSILON)
    )
    og[...] = gradient
    om[...] = masv[...] - LEARN_RATE * (corrected + WEIGHT_DECAY * masv[...])
    of[...] = new_first
    osn[...] = new_second
    for n, (a, b) in enumerate(((og, o_grad), (om, o_mas), (of, o_fst), (osn, o_snd))):
        cp = pltpu.make_async_copy(a, b, lsem.at[10 + n])
        cp.start()
        outs.append(cp)

    for src, i in sends:
        pltpu.make_async_copy(src, src, ssem.at[i]).wait()
    for k in range(4):
        src = rb.at[pl.ds(32 * k, 32)]

        @pl.when(jnp.logical_not(jnp.logical_and(is_self, k == r)))
        def _():
            pltpu.make_async_copy(src, src, ssem.at[o_id + k]).wait()
    for cp in outs:
        cp.wait()


N_SEM = 48


def per_device(act, que, key, gout, seg, wgt, mas, fst, snd):
    sds = jax.ShapeDtypeStruct
    any_spec = pl.BlockSpec(memory_space=pl.ANY)
    vm = pltpu.VMEM
    shard = (QTR, HD)
    return pl.pallas_call(
        kernel,
        out_shape=(
            sds((TOK, HALF), BF16), sds((TOK, HD), BF16),
            sds(shard, F32), sds(shard, F32), sds(shard, F32), sds(shard, F32),
        ),
        in_specs=[any_spec] * 9,
        out_specs=[any_spec] * 6,
        scratch_shapes=[
            vm((2 * TOK, HALF), BF16),
            vm((TOK, HEADS * HD), BF16), vm((TOK, HD), BF16), vm((TOK, HEADS * HD), BF16),
            vm((1, TOK), jnp.int32), vm(shard, F32), vm(shard, F32), vm(shard, F32),
            vm((4, QTR, 4 * HD), BF16),
            vm((TOK, TOK), F32),
            vm((HEADS, TOK, TOK), F32),
            vm((TOK, HD), F32),
            vm((4 * HD, 2 * TOK), BF16),
            vm((6, 2 * HD, QTR), BF16),
            vm((2, 2 * HD, QTR), F32),
            vm((6, 2 * HD, QTR), BF16),
            vm((4 * HD, QTR), F32),
            vm((6, HD, QTR), BF16),
            vm((HD, QTR), BF16),
            vm((4, 32, QTR), BF16),
            vm((HD, QTR), F32),
            vm((2 * TOK, 4 * HD), F32),
            vm((TOK, 4 * HD), F32),
            vm((TOK, 4 * HD), BF16),
            vm((3, TOK, HD), BF16),
            vm((TOK, HD), BF16),
            vm((HD, TOK), BF16),
            vm((TOK, HD), F32),
            vm((TOK, HEADS * HD), BF16), vm((TOK, HD), BF16),
            vm(shard, F32), vm(shard, F32), vm(shard, F32), vm(shard, F32),
            pltpu.SemaphoreType.DMA((N_SEM,)),
            pltpu.SemaphoreType.DMA((N_SEM,)),
            pltpu.SemaphoreType.DMA((16,)),
        ],
        compiler_params=pltpu.CompilerParams(
            collective_id=0, has_side_effects=True, vmem_limit_bytes=40 << 20
        ),
    )(act, que, key, gout, seg.reshape(1, TOK), wgt, mas, fst, snd)


def solution(mesh):
    token = P(("shard", "replica"), "tensor")
    row = P("shard", "tensor")
    return jax.shard_map(
        per_device,
        mesh=mesh,
        in_specs=(token, token, token, token, P(("shard", "replica")), row, row, row, row),
        out_specs=(token, token, row, row, row, row),
        check_vma=False,
    )
```

```python
import functools
import math

import jax
import jax.numpy as jnp
from jax import lax
from jax.experimental import pallas as pl
from jax.experimental.pallas import tpu as pltpu
from jax.sharding import PartitionSpec as P

STEP = 10
BETA_FIRST = 0.9
BETA_SECOND = 0.95
LEARN_RATE = 0.001
WEIGHT_DECAY = 0.1
EPSILON = 1e-08

F32 = jnp.float32
BF16 = jnp.bfloat16
MESH = pl.DeviceIdType.MESH
TOK = 256
HD = 128
HEADS = 8
HALF = 1024
QTR = 256
RANKS = 128
FACTOR = 1.0 / math.sqrt(HD)
NT = (((1,), (1,)), ((), ()))


def place(x, y, z, c):
    return (y, (x // 2) * 16 + z, (x % 2) * 2 + c)


def kernel(
    act, que, key, gout, seg, wgt, mas, fst, snd,
    o_gq, o_gk, o_grad, o_mas, o_fst, o_snd,
    a2, qv, kv, gov, segv, masv, fstv, sndv,
    wbuf, bias, wst, gv, gt, tt, tmg, r1, sx, zr, rb, ob, gf,
    pp, pr, vs, vr, vals, ktr, gk, gqv, gkv, og, om, of, osn,
    ssem, rsem, lsem,
):
    y = lax.axis_index("tensor")
    s = lax.axis_index("shard")
    r = lax.axis_index("replica")
    z = s % 16
    c = r % 2
    x = (s // 16) * 2 + r // 2

    ids = [0]

    def new_id(n=1):
        ids[0] += n
        return ids[0] - n

    def send(src, dst, i, dev):
        cp = pltpu.make_async_remote_copy(
            src_ref=src, dst_ref=dst, send_sem=ssem.at[i], recv_sem=rsem.at[i],
            device_id=dev, device_id_type=MESH,
        )
        cp.start()
        sends.append((src, i))

    def got(ref, i):
        pltpu.make_async_copy(ref, ref, rsem.at[i]).wait()

    sends = []
    xr, xl = (x + 1) % 4, (x + 3) % 4
    xo = (x + 2) % 4
    c_dev = place(x, y, z, 1 - c)
    xr_dev, xl_dev = place(xr, y, z, c), place(xl, y, z, c)

    def y_dev(d):
        return place(x, (y + d) % 4, z, c)

    def z_dev(d):
        return place(x, y, (z + d + 16) % 16, c)

    s_y, s_c, s_q = s // 8, (s % 8) // 4, s % 4
    own_q = z % 4
    own_s, own_y = 8 * y + 4 * c + own_q, x

    def rep_dev(k):
        return place(y, s_y, 4 * k + s_q, s_c)

    def owner_dev(k):
        return (own_y, own_s, k)

    is_self = jnp.logical_and(own_s == s, own_y == y)

    barrier = pltpu.get_barrier_semaphore()
    for dev in [c_dev, xr_dev, xl_dev, place(x + 1 - 2 * (x % 2), y, z, 1 - c)] + [
        y_dev(d) for d in (1, 2, 3)
    ] + [z_dev(d) for d in (-2, -1, 1, 2)]:
        pl.semaphore_signal(barrier, inc=1, device_id=dev, device_id_type=MESH)
    for k in range(4):
        @pl.when(jnp.logical_not(jnp.logical_and(is_self, k == r)))
        def _():
            pl.semaphore_signal(barrier, inc=1, device_id=owner_dev(k), device_id_type=MESH)

        @pl.when(jnp.logical_not(jnp.logical_and(is_self, k == z // 4)))
        def _():
            pl.semaphore_signal(barrier, inc=1, device_id=rep_dev(k), device_id_type=MESH)

    mine = pl.ds(pl.multiple_of(TOK * c, TOK), TOK)
    theirs = pl.ds(pl.multiple_of(TOK * (1 - c), TOK), TOK)
    loads = [
        (que, qv), (key, kv), (seg, segv), (gout, gov),
        (act.at[:, pl.ds(pl.multiple_of(HALF * c, HALF), HALF)], a2.at[mine]),
        (mas, masv), (fst, fstv), (snd, sndv),
    ]
    copies = [pltpu.make_async_copy(a, b, lsem.at[n]) for n, (a, b) in enumerate(loads)]
    for cp in copies:
        cp.start()

    for cp in copies[:4]:
        cp.wait()
    seg_row = jnp.broadcast_to(segv[...].astype(F32), (TOK, TOK))
    rows = lax.broadcasted_iota(jnp.int32, (TOK, TOK), 0)
    cols = lax.broadcasted_iota(jnp.int32, (TOK, TOK), 1)
    allowed = jnp.logical_and(seg_row.T == seg_row, rows <= cols)
    bias[...] = jnp.where(allowed, 0.0, -1e30)
    ktr[...] = kv[...].astype(F32).T.astype(BF16)

    def forward_head(h, acc):
        lanes = pl.ds(pl.multiple_of(h * HD, HD), HD)
        scores = lax.dot_general(kv[...], qv[:, lanes], NT, preferred_element_type=F32)
        scores = scores * FACTOR + bias[...]
        powered = jnp.exp(scores - jnp.max(scores, axis=0, keepdims=True))
        weights = powered * (1.0 / jnp.sum(powered, axis=0, keepdims=True))
        wst[h] = weights
        return acc + jnp.dot(weights.astype(BF16), gov[:, lanes], preferred_element_type=F32)

    acc = lax.fori_loop(0, HEADS, forward_head, jnp.zeros((TOK, HD), F32))
    gyt = pl.ds(pl.multiple_of(HD * y, HD), HD)
    gt[gyt, mine] = acc.T.astype(BF16)

    pl.semaphore_wait(barrier, 19 - 2 * is_self.astype(jnp.int32))

    g_y = new_id(3)
    for d in (2, 1, 3):
        send(gt.at[gyt, mine], gt.at[gyt, mine], g_y + d - 1, y_dev(d))
    g_c = new_id(4)
    send(gt.at[gyt, mine], gt.at[gyt, mine], g_c, c_dev)

    w1a = new_id()
    step = (r - 2 * (y % 2) - s_c + 9) % 4
    send(
        wgt, wbuf.at[y, pl.ds(pl.multiple_of(QTR * s_q, QTR), QTR)], w1a,
        place(y, s_y, (z + 4 * step) % 16, s_c),
    )
    a_id = new_id()
    send(act.at[:, pl.ds(pl.multiple_of(HALF * (1 - c), HALF), HALF)], a2.at[mine], a_id, c_dev)

    for d in (1, 3, 2):
        rows_d = pl.ds(pl.multiple_of(HD * ((y - d + 4) % 4), HD), HD)
        got(gt.at[rows_d, mine], g_y + d - 1)
        send(gt.at[rows_d, mine], gt.at[rows_d, mine], g_c + d, c_dev)
    copies[4].wait()
    got(a2.at[theirs], a_id)
    for n in range(4):
        rows_d = pl.ds(pl.multiple_of(HD * ((y - n + 4) % 4), HD), HD)
        got(gt.at[rows_d, theirs], g_c + n)

    def term(q, half):
        return jnp.dot(
            gt[pl.ds(pl.multiple_of(HD * q, HD), HD), :],
            a2[:, HALF // 2 * half : HALF // 2 * (half + 1)],
            preferred_element_type=F32,
        )

    r1_id = new_id(6)
    tt[0] = term(xo, 0).astype(BF16)
    send(tt.at[0], r1.at[0], r1_id, xr_dev)
    tt[1] = term(xo, 1).astype(BF16)
    send(tt.at[1], r1.at[1], r1_id + 1, xl_dev)
    tt[2] = term(xr, 1).astype(BF16)
    send(tt.at[2], r1.at[2], r1_id + 2, xr_dev)
    tt[3] = term(xl, 0).astype(BF16)
    send(tt.at[3], r1.at[3], r1_id + 3, xl_dev)
    tmg[0] = term(xr, 0)
    tmg[1] = term(xl, 1)

    def quarter_of(q):
        return pl.ds(pl.multiple_of(QTR * (q % 4), QTR), QTR)

    side = 1 - 2 * (z % 2)
    mine_q = wbuf.at[x, quarter_of(own_q)]
    got(mine_q, w1a)
    w1b = new_id(3)
    send(mine_q, mine_q, w1b, z_dev(2 * side))
    send(mine_q, mine_q, w1b + 1, z_dev(1))
    send(mine_q, mine_q, w1b + 2, z_dev(-1))

    top, bot = slice(0, HALF // 2), slice(HALF // 2, HALF)
    sx[:, top] = term(x, 0)
    sx[:, bot] = term(x, 1)
    got(r1.at[0], r1_id)
    tt[4] = (tmg[0] + r1[0].astype(F32)).astype(BF16)
    send(tt.at[4], r1.at[4], r1_id + 4, xr_dev)
    got(r1.at[1], r1_id + 1)
    tt[5] = (tmg[1] + r1[1].astype(F32)).astype(BF16)
    send(tt.at[5], r1.at[5], r1_id + 5, xl_dev)

    got(wbuf.at[x, quarter_of(z - 1 + 4)], w1b + 1)
    got(wbuf.at[x, quarter_of(z + 1)], w1b + 2)
    got(wbuf.at[x, quarter_of(z + 2)], w1b)
    lo, hi = pl.ds(0, HALF // 2), pl.ds(HALF // 2, HALF // 2)
    w2 = new_id(6)
    send(wbuf.at[x, lo], wbuf.at[x, lo], w2, xr_dev)
    send(wbuf.at[x, hi], wbuf.at[x, hi], w2 + 1, xl_dev)
    send(wbuf.at[x, hi], wbuf.at[x, hi], w2 + 2, xr_dev)
    send(wbuf.at[x, lo], wbuf.at[x, lo], w2 + 3, xl_dev)

    v1 = new_id(4)

    def values_of(q, n):
        pp[q] = jnp.dot(a2[...], wbuf[q], preferred_element_type=F32)
        send(pp.at[q, theirs], pr.at[q], v1 + n, c_dev)

    got(r1.at[3], r1_id + 3)
    got(r1.at[2], r1_id + 2)
    got(r1.at[4], r1_id + 4)
    got(r1.at[5], r1_id + 5)
    sx[:, top] = sx[:, top] + (r1[3].astype(F32) + r1[4].astype(F32))
    sx[:, bot] = sx[:, bot] + (r1[2].astype(F32) + r1[5].astype(F32))
    z_id = new_id(3)
    for n, d in enumerate((-2 * side, 1, -1)):
        zr[3 + n] = sx[:, quarter_of(z + d + 16)].astype(BF16)
        send(zr.at[3 + n], zr.at[n], z_id + n, z_dev(d))

    values_of(x, 0)
    got(wbuf.at[xl, lo], w2)
    send(wbuf.at[xl, lo], wbuf.at[xl, lo], w2 + 4, xr_dev)
    got(wbuf.at[xr, hi], w2 + 1)
    send(wbuf.at[xr, hi], wbuf.at[xr, hi], w2 + 5, xl_dev)

    for n in range(3):
        got(zr.at[n], z_id + n)
    rb[...] = (
        sx[:, quarter_of(own_q)]
        + zr[0].astype(F32) + zr[1].astype(F32) + zr[2].astype(F32)
    ).astype(BF16)
    o_id = new_id(4)
    for k in range(4):
        src = rb.at[pl.ds(32 * k, 32)]
        stay = jnp.logical_and(is_self, k == r)

        @pl.when(jnp.logical_not(stay))
        def _():
            pltpu.make_async_remote_copy(
                src_ref=src, dst_ref=ob.at[z // 4], send_sem=ssem.at[o_id + k],
                recv_sem=rsem.at[o_id + z // 4], device_id=owner_dev(k), device_id_type=MESH,
            ).start()

        @pl.when(stay)
        def _():
            pltpu.make_async_copy(src, ob.at[z // 4], rsem.at[o_id + z // 4]).start()

    got(wbuf.at[xl, hi], w2 + 2)
    values_of(xl, 1)
    got(wbuf.at[xr, lo], w2 + 3)
    values_of(xr, 2)
    got(wbuf.at[xo, lo], w2 + 4)
    got(wbuf.at[xo, hi], w2 + 5)
    values_of(xo, 3)

    for n, q in ((0, x), (2, xl), (1, xr), (3, xo)):
        got(pr.at[q], v1 + n)
    v2 = new_id(3)
    for d in (2, 1, 3):
        q = (y + d) % 4
        vs[d - 1] = (pp[q, mine] + pr[q]).astype(BF16)
        send(vs.at[d - 1], vr.at[d - 1], v2 + d - 1, y_dev(d))

    for k in range(4):
        got(ob.at[k], o_id + k)
    quarter = pl.ds(pl.multiple_of(32 * r, 32), 32)
    gf[quarter, :] = (
        ob[0].astype(F32) + ob[1].astype(F32) + ob[2].astype(F32) + ob[3].astype(F32)
    ) * (1.0 / RANKS)
    f_id = new_id(3)
    for d in (1, 2, 3):
        rd = (r + d) % 4
        send(gf.at[quarter], gf.at[quarter], f_id + d - 1, (y, s, rd))

    for d in (1, 2, 3):
        got(vr.at[d - 1], v2 + d - 1)
    vals[...] = (
        pp[y, mine] + pr[y] + vr[0].astype(F32) + vr[1].astype(F32) + vr[2].astype(F32)
    ).astype(BF16)

    def backward_head(h, acc):
        lanes = pl.ds(pl.multiple_of(h * HD, HD), HD)
        gw = lax.dot_general(vals[...], gov[:, lanes], NT, preferred_element_type=F32)
        weights = wst[h]
        dots = jnp.sum(weights.astype(BF16).astype(F32) * gw, axis=0, keepdims=True)
        gs = (weights * (gw - dots) * FACTOR).astype(BF16)
        gq = jnp.dot(ktr[...], gs, preferred_element_type=F32)
        gqv[:, lanes] = gq.T.astype(BF16)
        return acc + jnp.dot(gs, qv[:, lanes], preferred_element_type=F32)

    gkv[...] = lax.fori_loop(0, HEADS, backward_head, jnp.zeros((TOK, HD), F32)).astype(BF16)
    outs = [pltpu.make_async_copy(gqv, o_gq, lsem.at[8]), pltpu.make_async_copy(gkv, o_gk, lsem.at[9])]
    for cp in outs:
        cp.start()

    for d in (1, 2, 3):
        other = pl.ds(pl.multiple_of(32 * ((r - d + 4) % 4), 32), 32)
        got(gf.at[other], f_id + d - 1)
    for cp in copies[5:]:
        cp.wait()
    gradient = gf[...].T
    new_first = BETA_FIRST * fstv[...] + (1.0 - BETA_FIRST) * gradient
    new_second = BETA_SECOND * sndv[...] + (1.0 - BETA_SECOND) * gradient * gradient
    corrected = (
        new_first
        / (1.0 - BETA_FIRST**STEP)
        / (jnp.sqrt(new_second / (1.0 - BETA_SECOND**STEP)) + EPSILON)
    )
    og[...] = gradient
    om[...] = masv[...] - LEARN_RATE * (corrected + WEIGHT_DECAY * masv[...])
    of[...] = new_first
    osn[...] = new_second
    for n, (a, b) in enumerate(((og, o_grad), (om, o_mas), (of, o_fst), (osn, o_snd))):
        cp = pltpu.make_async_copy(a, b, lsem.at[10 + n])
        cp.start()
        outs.append(cp)

    for src, i in sends:
        pltpu.make_async_copy(src, src, ssem.at[i]).wait()
    for k in range(4):
        src = rb.at[pl.ds(32 * k, 32)]

        @pl.when(jnp.logical_not(jnp.logical_and(is_self, k == r)))
        def _():
            pltpu.make_async_copy(src, src, ssem.at[o_id + k]).wait()
    for cp in outs:
        cp.wait()


N_SEM = 48


def per_device(act, que, key, gout, seg, wgt, mas, fst, snd):
    sds = jax.ShapeDtypeStruct
    any_spec = pl.BlockSpec(memory_space=pl.ANY)
    vm = pltpu.VMEM
    shard = (QTR, HD)
    return pl.pallas_call(
        kernel,
        out_shape=(
            sds((TOK, HALF), BF16), sds((TOK, HD), BF16),
            sds(shard, F32), sds(shard, F32), sds(shard, F32), sds(shard, F32),
        ),
        in_specs=[any_spec] * 9,
        out_specs=[any_spec] * 6,
        scratch_shapes=[
            vm((2 * TOK, HALF), BF16),
            vm((TOK, HEADS * HD), BF16), vm((TOK, HD), BF16), vm((TOK, HEADS * HD), BF16),
            vm((1, TOK), jnp.int32), vm(shard, F32), vm(shard, F32), vm(shard, F32),
            vm((4, HALF, HD), BF16),
            vm((TOK, TOK), F32),
            vm((HEADS, TOK, TOK), F32),
            vm((TOK, HD), F32),
            vm((4 * HD, 2 * TOK), BF16),
            vm((6, HD, HALF // 2), BF16),
            vm((2, HD, HALF // 2), F32),
            vm((6, HD, HALF // 2), BF16),
            vm((HD, HALF), F32),
            vm((6, HD, QTR), BF16),
            vm((HD, QTR), BF16),
            vm((4, 32, QTR), BF16),
            vm((HD, QTR), F32),
            vm((4, 2 * TOK, HD), F32),
            vm((4, TOK, HD), F32),
            vm((3, TOK, HD), BF16),
            vm((3, TOK, HD), BF16),
            vm((TOK, HD), BF16),
            vm((HD, TOK), BF16),
            vm((TOK, HD), F32),
            vm((TOK, HEADS * HD), BF16), vm((TOK, HD), BF16),
            vm(shard, F32), vm(shard, F32), vm(shard, F32), vm(shard, F32),
            pltpu.SemaphoreType.DMA((N_SEM,)),
            pltpu.SemaphoreType.DMA((N_SEM,)),
            pltpu.SemaphoreType.DMA((16,)),
        ],
        compiler_params=pltpu.CompilerParams(
            collective_id=0, has_side_effects=True, vmem_limit_bytes=60 << 20
        ),
    )(act, que, key, gout, seg.reshape(1, TOK), wgt, mas, fst, snd)


def solution(mesh):
    token = P(("shard", "replica"), "tensor")
    row = P("shard", "tensor")
    return jax.shard_map(
        per_device,
        mesh=mesh,
        in_specs=(token, token, token, token, P(("shard", "replica")), row, row, row, row),
        out_specs=(token, token, row, row, row, row),
        check_vma=False,
    )
```

```python
import functools
import math

import jax
import jax.numpy as jnp
from jax import lax
from jax.experimental import pallas as pl
from jax.experimental.pallas import tpu as pltpu
from jax.sharding import PartitionSpec as P

STEP = 10
BETA_FIRST = 0.9
BETA_SECOND = 0.95
LEARN_RATE = 0.001
WEIGHT_DECAY = 0.1
EPSILON = 1e-08

F32 = jnp.float32
BF16 = jnp.bfloat16
MESH = pl.DeviceIdType.MESH
TOK = 256
HD = 128
HEADS = 8
HALF = 1024
QTR = 256
RANKS = 128
CH = 64
FACTOR = 1.0 / math.sqrt(HD)
NT = (((1,), (1,)), ((), ()))


def place(x, y, z, c):
    return (y, (x // 2) * 16 + z, (x % 2) * 2 + c)


def kernel(
    act, que, key, gout, seg, wgt, mas, fst, snd,
    o_gq, o_gk, o_grad, o_mas, o_fst, o_snd,
    a2, qv, kv, gov, segv, masv, fstv, sndv,
    wbuf, bias, wst, gv, gt, tt, tmg, r1, sx, zr, rb, ob, gf,
    pp, pr, vs, vr, vals, ktr, gk, gqv, gkv, og, om, of, osn,
    ssem, rsem, lsem,
):
    y = lax.axis_index("tensor")
    s = lax.axis_index("shard")
    r = lax.axis_index("replica")
    z = s % 16
    c = r % 2
    x = (s // 16) * 2 + r // 2

    ids = [0]

    def new_id(n=1):
        ids[0] += n
        return ids[0] - n

    def send(src, dst, i, dev):
        cp = pltpu.make_async_remote_copy(
            src_ref=src, dst_ref=dst, send_sem=ssem.at[i], recv_sem=rsem.at[i],
            device_id=dev, device_id_type=MESH,
        )
        cp.start()
        sends.append((src, i))

    def got(ref, i):
        pltpu.make_async_copy(ref, ref, rsem.at[i]).wait()

    sends = []
    xr, xl = (x + 1) % 4, (x + 3) % 4
    xo = (x + 2) % 4
    c_dev = place(x, y, z, 1 - c)
    xr_dev, xl_dev = place(xr, y, z, c), place(xl, y, z, c)

    def y_dev(d):
        return place(x, (y + d) % 4, z, c)

    def z_dev(d):
        return place(x, y, (z + d + 16) % 16, c)

    s_y, s_c, s_q = s // 8, (s % 8) // 4, s % 4
    own_q = z % 4
    own_s, own_y = 8 * y + 4 * c + own_q, x

    def rep_dev(k):
        return place(y, s_y, 4 * k + s_q, s_c)

    def owner_dev(k):
        return (own_y, own_s, k)

    is_self = jnp.logical_and(own_s == s, own_y == y)

    barrier = pltpu.get_barrier_semaphore()
    for dev in [c_dev, xr_dev, xl_dev, place(x + 1 - 2 * (x % 2), y, z, 1 - c)] + [
        y_dev(d) for d in (1, 2, 3)
    ] + [z_dev(d) for d in (-2, -1, 1, 2)]:
        pl.semaphore_signal(barrier, inc=1, device_id=dev, device_id_type=MESH)
    for k in range(4):
        @pl.when(jnp.logical_not(jnp.logical_and(is_self, k == r)))
        def _():
            pl.semaphore_signal(barrier, inc=1, device_id=owner_dev(k), device_id_type=MESH)

        @pl.when(jnp.logical_not(jnp.logical_and(is_self, k == z // 4)))
        def _():
            pl.semaphore_signal(barrier, inc=1, device_id=rep_dev(k), device_id_type=MESH)

    mine = pl.ds(pl.multiple_of(TOK * c, TOK), TOK)
    theirs = pl.ds(pl.multiple_of(TOK * (1 - c), TOK), TOK)
    loads = [
        (que, qv), (key, kv), (seg, segv), (gout, gov),
        (act.at[:, pl.ds(pl.multiple_of(HALF * c, HALF), HALF)], a2.at[mine]),
        (mas, masv), (fst, fstv), (snd, sndv),
    ]
    copies = [pltpu.make_async_copy(a, b, lsem.at[n]) for n, (a, b) in enumerate(loads)]
    for cp in copies:
        cp.start()

    for cp in copies[:4]:
        cp.wait()
    seg_row = jnp.broadcast_to(segv[...].astype(F32), (TOK, TOK))
    rows = lax.broadcasted_iota(jnp.int32, (TOK, TOK), 0)
    cols = lax.broadcasted_iota(jnp.int32, (TOK, TOK), 1)
    allowed = jnp.logical_and(seg_row.T == seg_row, rows <= cols)
    bias[...] = jnp.where(allowed, 0.0, -1e30)
    ktr[...] = kv[...].astype(F32).T.astype(BF16)

    def forward_head(h, acc):
        lanes = pl.ds(pl.multiple_of(h * HD, HD), HD)
        scores = lax.dot_general(kv[...], qv[:, lanes], NT, preferred_element_type=F32)
        scores = scores * FACTOR + bias[...]
        powered = jnp.exp(scores - jnp.max(scores, axis=0, keepdims=True))
        weights = powered * (1.0 / jnp.sum(powered, axis=0, keepdims=True))
        wst[h] = weights
        return acc + jnp.dot(weights.astype(BF16), gov[:, lanes], preferred_element_type=F32)

    acc = lax.fori_loop(0, 6, forward_head, jnp.zeros((TOK, HD), F32), unroll=2)
    pl.semaphore_wait(barrier, 19 - 2 * is_self.astype(jnp.int32))

    w1a = new_id(2)
    step = (r - 2 * (y % 2) - s_c + 9) % 4
    for p in range(2):
        send(
            wgt.at[pl.ds(HD * p, HD)], wbuf.at[y, s_q, p], w1a + p,
            place(y, s_y, (z + 4 * step) % 16, s_c),
        )
    a_id = new_id()
    send(act.at[:, pl.ds(pl.multiple_of(HALF * (1 - c), HALF), HALF)], a2.at[mine], a_id, c_dev)

    acc = lax.fori_loop(6, HEADS, forward_head, acc, unroll=2)
    gyt = pl.ds(pl.multiple_of(HD * y, HD), HD)
    gt[gyt, mine] = acc.T.astype(BF16)
    g_y = new_id(3)
    for d in (2, 1, 3):
        send(gt.at[gyt, mine], gt.at[gyt, mine], g_y + d - 1, y_dev(d))
    g_c = new_id(4)
    send(gt.at[gyt, mine], gt.at[gyt, mine], g_c, c_dev)

    for d in (1, 3, 2):
        rows_d = pl.ds(pl.multiple_of(HD * ((y - d + 4) % 4), HD), HD)
        got(gt.at[rows_d, mine], g_y + d - 1)
        send(gt.at[rows_d, mine], gt.at[rows_d, mine], g_c + d, c_dev)
    copies[4].wait()
    got(a2.at[theirs], a_id)
    for n in range(4):
        rows_d = pl.ds(pl.multiple_of(HD * ((y - n + 4) % 4), HD), HD)
        got(gt.at[rows_d, theirs], g_c + n)

    halves = (slice(0, HALF // 2), slice(HALF // 2, HALF))

    def term(q, p, half):
        return jnp.dot(
            gt[pl.ds(pl.multiple_of(HD * q + CH * p, CH), CH), :],
            a2[:, halves[half]],
            preferred_element_type=F32,
        )

    r1_id = new_id(12)

    def send_term(p, n, block, dev):
        tt[p, n] = block.astype(BF16)
        send(tt.at[p, n], r1.at[p, n], r1_id + 6 * p + n, dev)

    for p in range(2):
        send_term(p, 0, term(xo, p, 0), xr_dev)
        send_term(p, 1, term(xo, p, 1), xl_dev)
    for p in range(2):
        send_term(p, 2, term(xr, p, 1), xr_dev)
        send_term(p, 3, term(xl, p, 0), xl_dev)
        tmg[p, 0] = term(xr, p, 0)
        tmg[p, 1] = term(xl, p, 1)

    side = 1 - 2 * (z % 2)
    w1b = new_id(6)
    for p in range(2):
        mine_q = wbuf.at[x, own_q, p]
        got(mine_q, w1a + p)
        send(mine_q, mine_q, w1b + 3 * p, z_dev(2 * side))
        send(mine_q, mine_q, w1b + 3 * p + 1, z_dev(1))
        send(mine_q, mine_q, w1b + 3 * p + 2, z_dev(-1))

    for p in range(2):
        sx[p, :, halves[0]] = term(x, p, 0)
        sx[p, :, halves[1]] = term(x, p, 1)
    for p in range(2):
        got(r1.at[p, 0], r1_id + 6 * p)
        send_term(p, 4, tmg[p, 0] + r1[p, 0].astype(F32), xr_dev)
        got(r1.at[p, 1], r1_id + 6 * p + 1)
        send_term(p, 5, tmg[p, 1] + r1[p, 1].astype(F32), xl_dev)

    w2 = new_id(12)
    lo, hi = pl.ds(0, 2), pl.ds(2, 2)

    def send_block(q, part, p, n, dev):
        ref = wbuf.at[q, part, p]
        send(ref, ref, w2 + 6 * p + n, dev)

    for p in range(2):
        got(wbuf.at[x, (z + 3) % 4, p], w1b + 3 * p + 1)
        got(wbuf.at[x, (z + 1) % 4, p], w1b + 3 * p + 2)
        got(wbuf.at[x, (z + 2) % 4, p], w1b + 3 * p)
        send_block(x, lo, p, 0, xr_dev)
        send_block(x, hi, p, 1, xl_dev)
    for p in range(2):
        send_block(x, hi, p, 2, xr_dev)
        send_block(x, lo, p, 3, xl_dev)

    def quarter_of(q):
        return pl.ds(pl.multiple_of(QTR * (q % 4), QTR), QTR)

    z_id = new_id(6)
    for p in range(2):
        for n in (3, 2, 4, 5):
            got(r1.at[p, n], r1_id + 6 * p + n)
        sx[p, :, halves[0]] += r1[p, 3].astype(F32) + r1[p, 4].astype(F32)
        sx[p, :, halves[1]] += r1[p, 2].astype(F32) + r1[p, 5].astype(F32)
        for n, d in enumerate((-2 * side, 1, -1)):
            zr[p, 3 + n] = sx[p, :, quarter_of(z + d + 16)].astype(BF16)
            send(zr.at[p, 3 + n], zr.at[p, n], z_id + 3 * p + n, z_dev(d))

    v1 = new_id(4)
    v2 = new_id(3)

    def values_of(q, n):
        pp[q] = jnp.dot(a2[...], wbuf[q].reshape(HALF, HD), preferred_element_type=F32)
        send(pp.at[q, theirs], pr.at[q], v1 + n, c_dev)

    def values_out(q, n):
        got(pr.at[q], v1 + n)
        d = (q - y + 4) % 4

        @pl.when(d != 0)
        def _():
            vs[d - 1] = (pp[q, mine] + pr[q]).astype(BF16)
            pltpu.make_async_remote_copy(
                src_ref=vs.at[d - 1], dst_ref=vr.at[d - 1], send_sem=ssem.at[v2 + d - 1],
                recv_sem=rsem.at[v2 + d - 1], device_id=y_dev(d), device_id_type=MESH,
            ).start()

    values_of(x, 0)
    for p in range(2):
        got(wbuf.at[xl, lo, p], w2 + 6 * p)
        send_block(xl, lo, p, 4, xr_dev)
        got(wbuf.at[xr, hi, p], w2 + 6 * p + 1)
        send_block(xr, hi, p, 5, xl_dev)
    values_out(x, 0)

    o_id = new_id(8)
    for p in range(2):
        for n in range(3):
            got(zr.at[p, n], z_id + 3 * p + n)
        rb[p] = (
            sx[p, :, quarter_of(own_q)]
            + zr[p, 0].astype(F32) + zr[p, 1].astype(F32) + zr[p, 2].astype(F32)
        ).astype(BF16)
        for k in range(4):
            src = rb.at[p, pl.ds(16 * k, 16)]
            stay = jnp.logical_and(is_self, k == r)

            @pl.when(jnp.logical_not(stay))
            def _():
                pltpu.make_async_remote_copy(
                    src_ref=src, dst_ref=ob.at[z // 4, p], send_sem=ssem.at[o_id + 4 * p + k],
                    recv_sem=rsem.at[o_id + 4 * p + z // 4], device_id=owner_dev(k),
                    device_id_type=MESH,
                ).start()

            @pl.when(stay)
            def _():
                pltpu.make_async_copy(src, ob.at[z // 4, p], rsem.at[o_id + 4 * p + z // 4]).start()

    for p in range(2):
        got(wbuf.at[xl, hi, p], w2 + 6 * p + 2)
        got(wbuf.at[xr, lo, p], w2 + 6 * p + 3)
    values_of(xl, 1)
    values_of(xr, 2)
    values_out(xl, 1)
    values_out(xr, 2)
    for p in range(2):
        got(wbuf.at[xo, lo, p], w2 + 6 * p + 4)
        got(wbuf.at[xo, hi, p], w2 + 6 * p + 5)
    values_of(xo, 3)
    values_out(xo, 3)

    for p in range(2):
        for k in range(4):
            got(ob.at[k, p], o_id + 4 * p + k)
    quarter = pl.ds(pl.multiple_of(16 * r, 16), 16)
    gf[:, quarter, :] = (
        ob[0].astype(F32) + ob[1].astype(F32) + ob[2].astype(F32) + ob[3].astype(F32)
    ) * (1.0 / RANKS)
    f_id = new_id(3)
    for d in (1, 2, 3):
        rd = (r + d) % 4
        send(gf.at[:, quarter], gf.at[:, quarter], f_id + d - 1, (y, s, rd))

    for d in (1, 2, 3):
        got(vr.at[d - 1], v2 + d - 1)
    vals[...] = (
        pp[y, mine] + pr[y] + vr[0].astype(F32) + vr[1].astype(F32) + vr[2].astype(F32)
    ).astype(BF16)

    def backward_head(h, acc):
        lanes = pl.ds(pl.multiple_of(h * HD, HD), HD)
        gw = lax.dot_general(vals[...], gov[:, lanes], NT, preferred_element_type=F32)
        weights = wst[h]
        dots = jnp.sum(weights.astype(BF16).astype(F32) * gw, axis=0, keepdims=True)
        gs = (weights * (gw - dots) * FACTOR).astype(BF16)
        gq = jnp.dot(ktr[...], gs, preferred_element_type=F32)
        gqv[:, lanes] = gq.T.astype(BF16)
        return acc + jnp.dot(gs, qv[:, lanes], preferred_element_type=F32)

    gkv[...] = lax.fori_loop(
        0, HEADS, backward_head, jnp.zeros((TOK, HD), F32), unroll=2
    ).astype(BF16)
    outs = [pltpu.make_async_copy(gqv, o_gq, lsem.at[8]), pltpu.make_async_copy(gkv, o_gk, lsem.at[9])]
    for cp in outs:
        cp.start()

    for d in (1, 2, 3):
        other = pl.ds(pl.multiple_of(16 * ((r - d + 4) % 4), 16), 16)
        got(gf.at[:, other], f_id + d - 1)
    for cp in copies[5:]:
        cp.wait()
    gradient = gf[...].reshape(HD, QTR).T
    new_first = BETA_FIRST * fstv[...] + (1.0 - BETA_FIRST) * gradient
    new_second = BETA_SECOND * sndv[...] + (1.0 - BETA_SECOND) * gradient * gradient
    corrected = (
        new_first
        / (1.0 - BETA_FIRST**STEP)
        / (jnp.sqrt(new_second / (1.0 - BETA_SECOND**STEP)) + EPSILON)
    )
    og[...] = gradient
    om[...] = masv[...] - LEARN_RATE * (corrected + WEIGHT_DECAY * masv[...])
    of[...] = new_first
    osn[...] = new_second
    for n, (a, b) in enumerate(((og, o_grad), (om, o_mas), (of, o_fst), (osn, o_snd))):
        cp = pltpu.make_async_copy(a, b, lsem.at[10 + n])
        cp.start()
        outs.append(cp)

    for src, i in sends:
        pltpu.make_async_copy(src, src, ssem.at[i]).wait()
    for d in (1, 2, 3):
        pltpu.make_async_copy(vs.at[d - 1], vs.at[d - 1], ssem.at[v2 + d - 1]).wait()
    for p in range(2):
        for k in range(4):
            src = rb.at[p, pl.ds(16 * k, 16)]

            @pl.when(jnp.logical_not(jnp.logical_and(is_self, k == r)))
            def _():
                pltpu.make_async_copy(src, src, ssem.at[o_id + 4 * p + k]).wait()
    for cp in outs:
        cp.wait()


def hand_over(*refs):
    src, dst, held, sem = refs[:6], refs[6:12], refs[12:18], refs[18]
    moves = []
    for n in range(6):
        rows = src[n].shape[0] // (4 if n == 0 else 1)
        moves += [(n, pl.ds(rows * k, rows)) for k in range(4 if n == 0 else 1)]
    into = [
        pltpu.make_async_copy(src[n].at[rows], held[n].at[rows], sem.at[0, i])
        for i, (n, rows) in enumerate(moves)
    ]
    out = [
        pltpu.make_async_copy(held[n].at[rows], dst[n].at[rows], sem.at[1, i])
        for i, (n, rows) in enumerate(moves)
    ]
    for cp in into:
        cp.start()
    for cp, after in zip(into, out):
        cp.wait()
        after.start()
    for cp in out:
        cp.wait()


N_SEM = 64


def per_device(act, que, key, gout, seg, wgt, mas, fst, snd):
    sds = jax.ShapeDtypeStruct
    any_spec = pl.BlockSpec(memory_space=pl.ANY)
    vm = pltpu.VMEM
    shard = (QTR, HD)
    results = pl.pallas_call(
        kernel,
        out_shape=(
            sds((TOK, HALF), BF16), sds((TOK, HD), BF16),
            sds(shard, F32), sds(shard, F32), sds(shard, F32), sds(shard, F32),
        ),
        in_specs=[any_spec] * 9,
        out_specs=[any_spec] * 6,
        scratch_shapes=[
            vm((2 * TOK, HALF), BF16),
            vm((TOK, HEADS * HD), BF16), vm((TOK, HD), BF16), vm((TOK, HEADS * HD), BF16),
            vm((1, TOK), jnp.int32), vm(shard, F32), vm(shard, F32), vm(shard, F32),
            vm((4, 4, 2, HD, HD), BF16),
            vm((TOK, TOK), F32),
            vm((HEADS, TOK, TOK), F32),
            vm((TOK, HD), F32),
            vm((4 * HD, 2 * TOK), BF16),
            vm((2, 6, CH, HALF // 2), BF16),
            vm((2, 2, CH, HALF // 2), F32),
            vm((2, 6, CH, HALF // 2), BF16),
            vm((2, CH, HALF), F32),
            vm((2, 6, CH, QTR), BF16),
            vm((2, CH, QTR), BF16),
            vm((4, 2, 16, QTR), BF16),
            vm((2, CH, QTR), F32),
            vm((4, 2 * TOK, HD), F32),
            vm((4, TOK, HD), F32),
            vm((3, TOK, HD), BF16),
            vm((3, TOK, HD), BF16),
            vm((TOK, HD), BF16),
            vm((HD, TOK), BF16),
            vm((TOK, HD), F32),
            vm((TOK, HEADS * HD), BF16), vm((TOK, HD), BF16),
            vm(shard, F32), vm(shard, F32), vm(shard, F32), vm(shard, F32),
            pltpu.SemaphoreType.DMA((N_SEM,)),
            pltpu.SemaphoreType.DMA((N_SEM,)),
            pltpu.SemaphoreType.DMA((16,)),
        ],
        compiler_params=pltpu.CompilerParams(
            collective_id=0, has_side_effects=True, vmem_limit_bytes=60 << 20
        ),
    )(act, que, key, gout, seg.reshape(1, TOK), wgt, mas, fst, snd)
    return pl.pallas_call(
        hand_over,
        out_shape=tuple(sds(v.shape, v.dtype) for v in results),
        in_specs=[any_spec] * 6,
        out_specs=[any_spec] * 6,
        scratch_shapes=[vm(v.shape, v.dtype) for v in results] + [pltpu.SemaphoreType.DMA((2, 9))],
        compiler_params=pltpu.CompilerParams(vmem_limit_bytes=60 << 20),
    )(*results)


def solution(mesh):
    token = P(("shard", "replica"), "tensor")
    row = P("shard", "tensor")
    return jax.shard_map(
        per_device,
        mesh=mesh,
        in_specs=(token, token, token, token, P(("shard", "replica")), row, row, row, row),
        out_specs=(token, token, row, row, row, row),
        check_vma=False,
    )
```

```python
import functools
import math

import jax
import jax.numpy as jnp
from jax import lax
from jax.experimental import pallas as pl
from jax.experimental.pallas import tpu as pltpu
from jax.sharding import PartitionSpec as P

STEP = 10
BETA_FIRST = 0.9
BETA_SECOND = 0.95
LEARN_RATE = 0.001
WEIGHT_DECAY = 0.1
EPSILON = 1e-08

F32 = jnp.float32
BF16 = jnp.bfloat16
MESH = pl.DeviceIdType.MESH
TOK = 256
HD = 128
HEADS = 8
HALF = 1024
QTR = 256
RANKS = 128
CH = 64
FACTOR = 1.0 / math.sqrt(HD)
NT = (((1,), (1,)), ((), ()))


def place(x, y, z, c):
    return (y, (x // 2) * 16 + z, (x % 2) * 2 + c)


def kernel(
    act, que, key, gout, seg, wgt, mas, fst, snd,
    o_gq, o_gk, o_grad, o_mas, o_fst, o_snd,
    a2, qv, kv, gov, segv, masv, fstv, sndv,
    wbuf, bias, wst, gv, gt, tt, tmg, r1, sx, zr, rb, ob, gf,
    pp, pr, vs, vr, vals, ktr, gk, gqv, gkv, og, om, of, osn,
    ssem, rsem, lsem,
):
    y = lax.axis_index("tensor")
    s = lax.axis_index("shard")
    r = lax.axis_index("replica")
    z = s % 16
    c = r % 2
    x = (s // 16) * 2 + r // 2

    ids = [0]

    def new_id(n=1):
        ids[0] += n
        return ids[0] - n

    def send(src, dst, i, dev):
        cp = pltpu.make_async_remote_copy(
            src_ref=src, dst_ref=dst, send_sem=ssem.at[i], recv_sem=rsem.at[i],
            device_id=dev, device_id_type=MESH,
        )
        cp.start()
        sends.append((src, i))

    def got(ref, i):
        pltpu.make_async_copy(ref, ref, rsem.at[i]).wait()

    sends = []
    xr, xl = (x + 1) % 4, (x + 3) % 4
    xo = (x + 2) % 4
    c_dev = place(x, y, z, 1 - c)
    xr_dev, xl_dev = place(xr, y, z, c), place(xl, y, z, c)

    def y_dev(d):
        return place(x, (y + d) % 4, z, c)

    def z_dev(d):
        return place(x, y, (z + d + 16) % 16, c)

    s_y, s_c, s_q = s // 8, (s % 8) // 4, s % 4
    own_q = (z + 2) % 4
    own_s, own_y = 8 * y + 4 * c + own_q, x

    def rep_dev(k):
        return place(y, s_y, 4 * k + (s_q + 2) % 4, s_c)

    def owner_dev(k):
        return (own_y, own_s, k)

    barrier = pltpu.get_barrier_semaphore()
    for dev in [c_dev, xr_dev, xl_dev, place(x + 1 - 2 * (x % 2), y, z, 1 - c)] + [
        y_dev(d) for d in (1, 2, 3)
    ] + [z_dev(d) for d in (-2, -1, 1, 2)]:
        pl.semaphore_signal(barrier, inc=1, device_id=dev, device_id_type=MESH)
    for k in range(4):
        pl.semaphore_signal(barrier, inc=1, device_id=owner_dev(k), device_id_type=MESH)
        pl.semaphore_signal(barrier, inc=1, device_id=rep_dev(k), device_id_type=MESH)

    mine = pl.ds(pl.multiple_of(TOK * c, TOK), TOK)
    theirs = pl.ds(pl.multiple_of(TOK * (1 - c), TOK), TOK)
    loads = [
        (que, qv), (key, kv), (seg, segv), (gout, gov),
        (act.at[:, pl.ds(pl.multiple_of(HALF * c, HALF), HALF)], a2.at[mine]),
        (mas, masv), (fst, fstv), (snd, sndv),
    ]
    copies = [pltpu.make_async_copy(a, b, lsem.at[n]) for n, (a, b) in enumerate(loads)]
    for cp in copies:
        cp.start()

    for cp in copies[:4]:
        cp.wait()
    seg_row = jnp.broadcast_to(segv[...].astype(F32), (TOK, TOK))
    rows = lax.broadcasted_iota(jnp.int32, (TOK, TOK), 0)
    cols = lax.broadcasted_iota(jnp.int32, (TOK, TOK), 1)
    allowed = jnp.logical_and(seg_row.T == seg_row, rows <= cols)
    bias[...] = jnp.where(allowed, 0.0, -1e30)
    ktr[...] = kv[...].astype(F32).T.astype(BF16)

    def forward_head(h, acc):
        lanes = pl.ds(pl.multiple_of(h * HD, HD), HD)
        scores = lax.dot_general(kv[...], qv[:, lanes], NT, preferred_element_type=F32)
        scores = scores * FACTOR + bias[...]
        powered = jnp.exp(scores - jnp.max(scores, axis=0, keepdims=True))
        weights = powered * (1.0 / jnp.sum(powered, axis=0, keepdims=True))
        wst[h] = weights
        return acc + jnp.dot(weights.astype(BF16), gov[:, lanes], preferred_element_type=F32)

    acc = lax.fori_loop(0, 6, forward_head, jnp.zeros((TOK, HD), F32), unroll=2)
    pl.semaphore_wait(barrier, 19)

    w1a = new_id(2)
    for p in range(2):
        send(
            wgt.at[pl.ds(HD * p, HD)], wbuf.at[y, s_q, p], w1a + p,
            place(y, s_y, (z + 2 + 4 * r) % 16, s_c),
        )
    a_id = new_id()
    send(act.at[:, pl.ds(pl.multiple_of(HALF * (1 - c), HALF), HALF)], a2.at[mine], a_id, c_dev)

    acc = lax.fori_loop(6, HEADS, forward_head, acc, unroll=2)
    gyt = pl.ds(pl.multiple_of(HD * y, HD), HD)
    gt[gyt, mine] = acc.T.astype(BF16)
    g_y = new_id(3)
    for d in (2, 1, 3):
        send(gt.at[gyt, mine], gt.at[gyt, mine], g_y + d - 1, y_dev(d))
    g_c = new_id(4)
    send(gt.at[gyt, mine], gt.at[gyt, mine], g_c, c_dev)

    for d in (1, 3, 2):
        rows_d = pl.ds(pl.multiple_of(HD * ((y - d + 4) % 4), HD), HD)
        got(gt.at[rows_d, mine], g_y + d - 1)
        send(gt.at[rows_d, mine], gt.at[rows_d, mine], g_c + d, c_dev)
    copies[4].wait()
    got(a2.at[theirs], a_id)
    for n in range(4):
        rows_d = pl.ds(pl.multiple_of(HD * ((y - n + 4) % 4), HD), HD)
        got(gt.at[rows_d, theirs], g_c + n)

    halves = (slice(0, HALF // 2), slice(HALF // 2, HALF))

    def term(q, p, half):
        return jnp.dot(
            gt[pl.ds(pl.multiple_of(HD * q + CH * p, CH), CH), :],
            a2[:, halves[half]],
            preferred_element_type=F32,
        )

    r1_id = new_id(12)

    def send_term(p, n, block, dev):
        tt[p, n] = block.astype(BF16)
        send(tt.at[p, n], r1.at[p, n], r1_id + 6 * p + n, dev)

    for p in range(2):
        send_term(p, 0, term(xo, p, 0), xr_dev)
        send_term(p, 1, term(xo, p, 1), xl_dev)
    for p in range(2):
        send_term(p, 2, term(xr, p, 1), xr_dev)
        send_term(p, 3, term(xl, p, 0), xl_dev)
        tmg[p, 0] = term(xr, p, 0)
        tmg[p, 1] = term(xl, p, 1)

    side = 1 - 2 * (z % 2)
    w1b = new_id(6)
    for p in range(2):
        mine_q = wbuf.at[x, own_q, p]
        got(mine_q, w1a + p)
        send(mine_q, mine_q, w1b + 3 * p, z_dev(2 * side))
        send(mine_q, mine_q, w1b + 3 * p + 1, z_dev(1))
        send(mine_q, mine_q, w1b + 3 * p + 2, z_dev(-1))

    for p in range(2):
        sx[p, :, halves[0]] = term(x, p, 0)
        sx[p, :, halves[1]] = term(x, p, 1)
    for p in range(2):
        got(r1.at[p, 0], r1_id + 6 * p)
        send_term(p, 4, tmg[p, 0] + r1[p, 0].astype(F32), xr_dev)
        got(r1.at[p, 1], r1_id + 6 * p + 1)
        send_term(p, 5, tmg[p, 1] + r1[p, 1].astype(F32), xl_dev)

    w2 = new_id(12)
    lo, hi = pl.ds(0, 2), pl.ds(2, 2)

    def send_block(q, part, p, n, dev):
        ref = wbuf.at[q, part, p]
        send(ref, ref, w2 + 6 * p + n, dev)

    for p in range(2):
        got(wbuf.at[x, (z + 1) % 4, p], w1b + 3 * p + 1)
        got(wbuf.at[x, (z + 3) % 4, p], w1b + 3 * p + 2)
        got(wbuf.at[x, z % 4, p], w1b + 3 * p)
        send_block(x, lo, p, 0, xr_dev)
        send_block(x, hi, p, 1, xl_dev)
    for p in range(2):
        send_block(x, hi, p, 2, xr_dev)
        send_block(x, lo, p, 3, xl_dev)

    def quarter_of(q):
        return pl.ds(pl.multiple_of(QTR * (q % 4), QTR), QTR)

    z_id = new_id(6)
    for p in range(2):
        for n in (3, 2, 4, 5):
            got(r1.at[p, n], r1_id + 6 * p + n)
        sx[p, :, halves[0]] += r1[p, 3].astype(F32) + r1[p, 4].astype(F32)
        sx[p, :, halves[1]] += r1[p, 2].astype(F32) + r1[p, 5].astype(F32)
        for n, d in enumerate((-2 * side, 1, -1)):
            zr[p, 3 + n] = sx[p, :, quarter_of(z + d + 18)].astype(BF16)
            send(zr.at[p, 3 + n], zr.at[p, n], z_id + 3 * p + n, z_dev(d))

    v1 = new_id(4)
    v2 = new_id(3)

    def values_of(q, n):
        pp[q] = jnp.dot(a2[...], wbuf[q].reshape(HALF, HD), preferred_element_type=F32)
        send(pp.at[q, theirs], pr.at[q], v1 + n, c_dev)

    def values_out(q, n):
        got(pr.at[q], v1 + n)
        d = (q - y + 4) % 4

        @pl.when(d != 0)
        def _():
            vs[d - 1] = (pp[q, mine] + pr[q]).astype(BF16)
            pltpu.make_async_remote_copy(
                src_ref=vs.at[d - 1], dst_ref=vr.at[d - 1], send_sem=ssem.at[v2 + d - 1],
                recv_sem=rsem.at[v2 + d - 1], device_id=y_dev(d), device_id_type=MESH,
            ).start()

    values_of(x, 0)
    o_id = new_id(8)
    for p in range(2):
        got(wbuf.at[xl, lo, p], w2 + 6 * p)
        send_block(xl, lo, p, 4, xr_dev)
        got(wbuf.at[xr, hi, p], w2 + 6 * p + 1)
        send_block(xr, hi, p, 5, xl_dev)
        for n in range(3):
            got(zr.at[p, n], z_id + 3 * p + n)
        rb[p] = (
            sx[p, :, quarter_of(own_q)]
            + zr[p, 0].astype(F32) + zr[p, 1].astype(F32) + zr[p, 2].astype(F32)
        ).astype(BF16)
        for k in range(4):
            pltpu.make_async_remote_copy(
                src_ref=rb.at[p, pl.ds(16 * k, 16)], dst_ref=ob.at[z // 4, p],
                send_sem=ssem.at[o_id + 4 * p + k], recv_sem=rsem.at[o_id + 4 * p + z // 4],
                device_id=owner_dev(k), device_id_type=MESH,
            ).start()

    values_out(x, 0)
    for p in range(2):
        got(wbuf.at[xl, hi, p], w2 + 6 * p + 2)
        got(wbuf.at[xr, lo, p], w2 + 6 * p + 3)
    values_of(xl, 1)
    values_of(xr, 2)
    values_out(xl, 1)
    values_out(xr, 2)
    for p in range(2):
        got(wbuf.at[xo, lo, p], w2 + 6 * p + 4)
        got(wbuf.at[xo, hi, p], w2 + 6 * p + 5)
    values_of(xo, 3)
    values_out(xo, 3)

    for p in range(2):
        for k in range(4):
            got(ob.at[k, p], o_id + 4 * p + k)
    quarter = pl.ds(pl.multiple_of(16 * r, 16), 16)
    gf[:, quarter, :] = (
        ob[0].astype(F32) + ob[1].astype(F32) + ob[2].astype(F32) + ob[3].astype(F32)
    ) * (1.0 / RANKS)
    f_id = new_id(3)
    for d in (1, 2, 3):
        rd = (r + d) % 4
        send(gf.at[:, quarter], gf.at[:, quarter], f_id + d - 1, (y, s, rd))

    for d in (1, 2, 3):
        got(vr.at[d - 1], v2 + d - 1)
    vals[...] = (
        pp[y, mine] + pr[y] + vr[0].astype(F32) + vr[1].astype(F32) + vr[2].astype(F32)
    ).astype(BF16)

    def backward_head(h, acc):
        lanes = pl.ds(pl.multiple_of(h * HD, HD), HD)
        gw = lax.dot_general(vals[...], gov[:, lanes], NT, preferred_element_type=F32)
        weights = wst[h]
        dots = jnp.sum(weights.astype(BF16).astype(F32) * gw, axis=0, keepdims=True)
        gs = (weights * (gw - dots) * FACTOR).astype(BF16)
        gq = jnp.dot(ktr[...], gs, preferred_element_type=F32)
        gqv[:, lanes] = gq.T.astype(BF16)
        return acc + jnp.dot(gs, qv[:, lanes], preferred_element_type=F32)

    gkv[...] = lax.fori_loop(
        0, HEADS, backward_head, jnp.zeros((TOK, HD), F32), unroll=2
    ).astype(BF16)
    outs = [pltpu.make_async_copy(gqv, o_gq, lsem.at[8]), pltpu.make_async_copy(gkv, o_gk, lsem.at[9])]
    for cp in outs:
        cp.start()

    for d in (1, 2, 3):
        other = pl.ds(pl.multiple_of(16 * ((r - d + 4) % 4), 16), 16)
        got(gf.at[:, other], f_id + d - 1)
    for cp in copies[5:]:
        cp.wait()
    gradient = gf[...].reshape(HD, QTR).T
    new_first = BETA_FIRST * fstv[...] + (1.0 - BETA_FIRST) * gradient
    new_second = BETA_SECOND * sndv[...] + (1.0 - BETA_SECOND) * gradient * gradient
    corrected = (
        new_first
        / (1.0 - BETA_FIRST**STEP)
        / (jnp.sqrt(new_second / (1.0 - BETA_SECOND**STEP)) + EPSILON)
    )
    og[...] = gradient
    om[...] = masv[...] - LEARN_RATE * (corrected + WEIGHT_DECAY * masv[...])
    of[...] = new_first
    osn[...] = new_second
    for n, (a, b) in enumerate(((og, o_grad), (om, o_mas), (of, o_fst), (osn, o_snd))):
        cp = pltpu.make_async_copy(a, b, lsem.at[10 + n])
        cp.start()
        outs.append(cp)

    for src, i in sends:
        pltpu.make_async_copy(src, src, ssem.at[i]).wait()
    for d in (1, 2, 3):
        pltpu.make_async_copy(vs.at[d - 1], vs.at[d - 1], ssem.at[v2 + d - 1]).wait()
    for p in range(2):
        for k in range(4):
            src = rb.at[p, pl.ds(16 * k, 16)]
            pltpu.make_async_copy(src, src, ssem.at[o_id + 4 * p + k]).wait()
    for cp in outs:
        cp.wait()


def hand_over(*refs):
    src, dst, held, sem = refs[:6], refs[6:12], refs[12:18], refs[18]
    moves = []
    for n in range(6):
        rows = src[n].shape[0] // (4 if n == 0 else 1)
        moves += [(n, pl.ds(rows * k, rows)) for k in range(4 if n == 0 else 1)]
    into = [
        pltpu.make_async_copy(src[n].at[rows], held[n].at[rows], sem.at[0, i])
        for i, (n, rows) in enumerate(moves)
    ]
    out = [
        pltpu.make_async_copy(held[n].at[rows], dst[n].at[rows], sem.at[1, i])
        for i, (n, rows) in enumerate(moves)
    ]
    for cp in into:
        cp.start()
    for cp, after in zip(into, out):
        cp.wait()
        after.start()
    for cp in out:
        cp.wait()


N_SEM = 64


def per_device(act, que, key, gout, seg, wgt, mas, fst, snd):
    sds = jax.ShapeDtypeStruct
    any_spec = pl.BlockSpec(memory_space=pl.ANY)
    vm = pltpu.VMEM
    shard = (QTR, HD)
    results = pl.pallas_call(
        kernel,
        out_shape=(
            sds((TOK, HALF), BF16), sds((TOK, HD), BF16),
            sds(shard, F32), sds(shard, F32), sds(shard, F32), sds(shard, F32),
        ),
        in_specs=[any_spec] * 9,
        out_specs=[any_spec] * 6,
        scratch_shapes=[
            vm((2 * TOK, HALF), BF16),
            vm((TOK, HEADS * HD), BF16), vm((TOK, HD), BF16), vm((TOK, HEADS * HD), BF16),
            vm((1, TOK), jnp.int32), vm(shard, F32), vm(shard, F32), vm(shard, F32),
            vm((4, 4, 2, HD, HD), BF16),
            vm((TOK, TOK), F32),
            vm((HEADS, TOK, TOK), F32),
            vm((TOK, HD), F32),
            vm((4 * HD, 2 * TOK), BF16),
            vm((2, 6, CH, HALF // 2), BF16),
            vm((2, 2, CH, HALF // 2), F32),
            vm((2, 6, CH, HALF // 2), BF16),
            vm((2, CH, HALF), F32),
            vm((2, 6, CH, QTR), BF16),
            vm((2, CH, QTR), BF16),
            vm((4, 2, 16, QTR), BF16),
            vm((2, CH, QTR), F32),
            vm((4, 2 * TOK, HD), F32),
            vm((4, TOK, HD), F32),
            vm((3, TOK, HD), BF16),
            vm((3, TOK, HD), BF16),
            vm((TOK, HD), BF16),
            vm((HD, TOK), BF16),
            vm((TOK, HD), F32),
            vm((TOK, HEADS * HD), BF16), vm((TOK, HD), BF16),
            vm(shard, F32), vm(shard, F32), vm(shard, F32), vm(shard, F32),
            pltpu.SemaphoreType.DMA((N_SEM,)),
            pltpu.SemaphoreType.DMA((N_SEM,)),
            pltpu.SemaphoreType.DMA((16,)),
        ],
        compiler_params=pltpu.CompilerParams(
            collective_id=0, has_side_effects=True, vmem_limit_bytes=60 << 20
        ),
    )(act, que, key, gout, seg.reshape(1, TOK), wgt, mas, fst, snd)
    return pl.pallas_call(
        hand_over,
        out_shape=tuple(sds(v.shape, v.dtype) for v in results),
        in_specs=[any_spec] * 6,
        out_specs=[any_spec] * 6,
        scratch_shapes=[vm(v.shape, v.dtype) for v in results] + [pltpu.SemaphoreType.DMA((2, 9))],
        compiler_params=pltpu.CompilerParams(vmem_limit_bytes=60 << 20),
    )(*results)


def solution(mesh):
    token = P(("shard", "replica"), "tensor")
    row = P("shard", "tensor")
    return jax.shard_map(
        per_device,
        mesh=mesh,
        in_specs=(token, token, token, token, P(("shard", "replica")), row, row, row, row),
        out_specs=(token, token, row, row, row, row),
        check_vma=False,
    )
```

```python
import functools
import math

import jax
import jax.numpy as jnp
from jax import lax
from jax.experimental import pallas as pl
from jax.experimental.pallas import tpu as pltpu
from jax.sharding import PartitionSpec as P

STEP = 10
BETA_FIRST = 0.9
BETA_SECOND = 0.95
LEARN_RATE = 0.001
WEIGHT_DECAY = 0.1
EPSILON = 1e-08

F32 = jnp.float32
BF16 = jnp.bfloat16
MESH = pl.DeviceIdType.MESH
TOK = 256
HD = 128
HEADS = 8
HALF = 1024
QTR = 256
RANKS = 128
CH = 64
FACTOR = 1.0 / math.sqrt(HD)
NT = (((1,), (1,)), ((), ()))


def place(x, y, z, c):
    return (y, (x // 2) * 16 + z, (x % 2) * 2 + c)


def kernel(
    act, que, key, gout, seg, wgt, mas, fst, snd,
    o_gq, o_gk, o_grad, o_mas, o_fst, o_snd,
    a2, qv, kv, gov, segv, masv, fstv, sndv,
    wbuf, bias, wst, gv, gt, tt, tmg, r1, sx, zr, rb, ob, gf,
    pp, pr, vs, vr, vals, ktr, gk, gqv, gkv, og, om, of, osn,
    ssem, rsem, lsem,
):
    y = lax.axis_index("tensor")
    s = lax.axis_index("shard")
    r = lax.axis_index("replica")
    z = s % 16
    c = r % 2
    x = (s // 16) * 2 + r // 2

    ids = [0]

    def new_id(n=1):
        ids[0] += n
        return ids[0] - n

    def send(src, dst, i, dev):
        cp = pltpu.make_async_remote_copy(
            src_ref=src, dst_ref=dst, send_sem=ssem.at[i], recv_sem=rsem.at[i],
            device_id=dev, device_id_type=MESH,
        )
        cp.start()
        sends.append((src, i))

    def got(ref, i):
        pltpu.make_async_copy(ref, ref, rsem.at[i]).wait()

    sends = []
    xr, xl = (x + 1) % 4, (x + 3) % 4
    xo = (x + 2) % 4
    c_dev = place(x, y, z, 1 - c)
    xr_dev, xl_dev = place(xr, y, z, c), place(xl, y, z, c)

    def y_dev(d):
        return place(x, (y + d) % 4, z, c)

    def z_dev(d):
        return place(x, y, (z + d + 16) % 16, c)

    s_y, s_c, s_q = s // 8, (s % 8) // 4, s % 4
    own_q = (z + 2) % 4
    own_s, own_y = 8 * y + 4 * c + own_q, x

    def rep_dev(k):
        return place(y, s_y, 4 * k + (s_q + 2) % 4, s_c)

    def owner_dev(k):
        return (own_y, own_s, k)

    barrier = pltpu.get_barrier_semaphore()
    for dev in [c_dev, xr_dev, xl_dev, place(x + 1 - 2 * (x % 2), y, z, 1 - c)] + [
        y_dev(d) for d in (1, 2, 3)
    ] + [z_dev(d) for d in (-2, -1, 1, 2)]:
        pl.semaphore_signal(barrier, inc=1, device_id=dev, device_id_type=MESH)
    for k in range(4):
        pl.semaphore_signal(barrier, inc=1, device_id=owner_dev(k), device_id_type=MESH)
        pl.semaphore_signal(barrier, inc=1, device_id=rep_dev(k), device_id_type=MESH)

    mine = pl.ds(pl.multiple_of(TOK * c, TOK), TOK)
    theirs = pl.ds(pl.multiple_of(TOK * (1 - c), TOK), TOK)
    loads = [
        (que, qv), (key, kv), (seg, segv), (gout, gov),
        (act.at[:, pl.ds(pl.multiple_of(HALF * c, HALF), HALF)], a2.at[mine]),
        (mas, masv), (fst, fstv), (snd, sndv),
    ]
    copies = [pltpu.make_async_copy(a, b, lsem.at[n]) for n, (a, b) in enumerate(loads)]
    for cp in copies:
        cp.start()

    for cp in copies[:4]:
        cp.wait()
    seg_row = jnp.broadcast_to(segv[...].astype(F32), (TOK, TOK))
    rows = lax.broadcasted_iota(jnp.int32, (TOK, TOK), 0)
    cols = lax.broadcasted_iota(jnp.int32, (TOK, TOK), 1)
    allowed = jnp.logical_and(seg_row.T == seg_row, rows <= cols)
    bias[...] = jnp.where(allowed, 0.0, -1e30)
    ktr[...] = kv[...].astype(F32).T.astype(BF16)

    def forward_head(h, acc):
        lanes = pl.ds(pl.multiple_of(h * HD, HD), HD)
        scores = lax.dot_general(kv[...], qv[:, lanes], NT, preferred_element_type=F32)
        scores = scores * FACTOR + bias[...]
        powered = jnp.exp(scores - jnp.max(scores, axis=0, keepdims=True))
        weights = powered * (1.0 / jnp.sum(powered, axis=0, keepdims=True))
        wst[h] = weights
        return acc + jnp.dot(weights.astype(BF16), gov[:, lanes], preferred_element_type=F32)

    acc = lax.fori_loop(0, HEADS, forward_head, jnp.zeros((TOK, HD), F32), unroll=2)
    pl.semaphore_wait(barrier, 19)

    w1a = new_id(2)
    for p in range(2):
        send(
            wgt.at[pl.ds(HD * p, HD)], wbuf.at[y, s_q, p], w1a + p,
            place(y, s_y, (z + 2 + 4 * r) % 16, s_c),
        )
    a_id = new_id()
    send(act.at[:, pl.ds(pl.multiple_of(HALF * (1 - c), HALF), HALF)], a2.at[mine], a_id, c_dev)

    gyt = pl.ds(pl.multiple_of(HD * y, HD), HD)
    gt[gyt, mine] = acc.T.astype(BF16)
    g_y = new_id(3)
    for d in (2, 1, 3):
        send(gt.at[gyt, mine], gt.at[gyt, mine], g_y + d - 1, y_dev(d))
    g_c = new_id(4)
    send(gt.at[gyt, mine], gt.at[gyt, mine], g_c, c_dev)

    for d in (1, 3, 2):
        rows_d = pl.ds(pl.multiple_of(HD * ((y - d + 4) % 4), HD), HD)
        got(gt.at[rows_d, mine], g_y + d - 1)
        send(gt.at[rows_d, mine], gt.at[rows_d, mine], g_c + d, c_dev)
    copies[4].wait()
    got(a2.at[theirs], a_id)
    for n in range(4):
        rows_d = pl.ds(pl.multiple_of(HD * ((y - n + 4) % 4), HD), HD)
        got(gt.at[rows_d, theirs], g_c + n)

    halves = (slice(0, HALF // 2), slice(HALF // 2, HALF))

    def term(q, p, half):
        return jnp.dot(
            gt[pl.ds(pl.multiple_of(HD * q + CH * p, CH), CH), :],
            a2[:, halves[half]],
            preferred_element_type=F32,
        )

    r1_id = new_id(12)

    def send_term(p, n, block, dev):
        tt[p, n] = block.astype(BF16)
        send(tt.at[p, n], r1.at[p, n], r1_id + 6 * p + n, dev)

    for p in range(2):
        send_term(p, 0, term(xo, p, 0), xr_dev)
        send_term(p, 1, term(xo, p, 1), xl_dev)
    for p in range(2):
        send_term(p, 2, term(xr, p, 1), xr_dev)
        send_term(p, 3, term(xl, p, 0), xl_dev)
        tmg[p, 0] = term(xr, p, 0)
        tmg[p, 1] = term(xl, p, 1)

    side = 1 - 2 * (z % 2)
    w1b = new_id(6)
    for p in range(2):
        mine_q = wbuf.at[x, own_q, p]
        got(mine_q, w1a + p)
        send(mine_q, mine_q, w1b + 3 * p, z_dev(2 * side))
        send(mine_q, mine_q, w1b + 3 * p + 1, z_dev(1))
        send(mine_q, mine_q, w1b + 3 * p + 2, z_dev(-1))

    for p in range(2):
        sx[p, :, halves[0]] = term(x, p, 0)
        sx[p, :, halves[1]] = term(x, p, 1)
    for p in range(2):
        got(r1.at[p, 0], r1_id + 6 * p)
        send_term(p, 4, tmg[p, 0] + r1[p, 0].astype(F32), xr_dev)
        got(r1.at[p, 1], r1_id + 6 * p + 1)
        send_term(p, 5, tmg[p, 1] + r1[p, 1].astype(F32), xl_dev)

    w2 = new_id(12)
    lo, hi = pl.ds(0, 2), pl.ds(2, 2)

    def send_block(q, part, p, n, dev):
        ref = wbuf.at[q, part, p]
        send(ref, ref, w2 + 6 * p + n, dev)

    for p in range(2):
        got(wbuf.at[x, (z + 1) % 4, p], w1b + 3 * p + 1)
        got(wbuf.at[x, (z + 3) % 4, p], w1b + 3 * p + 2)
        got(wbuf.at[x, z % 4, p], w1b + 3 * p)
        send_block(x, lo, p, 0, xr_dev)
        send_block(x, hi, p, 1, xl_dev)
    for p in range(2):
        send_block(x, hi, p, 2, xr_dev)
        send_block(x, lo, p, 3, xl_dev)

    def quarter_of(q):
        return pl.ds(pl.multiple_of(QTR * (q % 4), QTR), QTR)

    z_id = new_id(6)
    for p in range(2):
        for n in (3, 2, 4, 5):
            got(r1.at[p, n], r1_id + 6 * p + n)
        sx[p, :, halves[0]] += r1[p, 3].astype(F32) + r1[p, 4].astype(F32)
        sx[p, :, halves[1]] += r1[p, 2].astype(F32) + r1[p, 5].astype(F32)
        for n, d in enumerate((-2 * side, 1, -1)):
            zr[p, 3 + n] = sx[p, :, quarter_of(z + d + 18)].astype(BF16)
            send(zr.at[p, 3 + n], zr.at[p, n], z_id + 3 * p + n, z_dev(d))

    v1 = new_id(4)
    v2 = new_id(3)

    def values_of(q, n):
        pp[q] = jnp.dot(a2[...], wbuf[q].reshape(HALF, HD), preferred_element_type=F32)
        send(pp.at[q, theirs], pr.at[q], v1 + n, c_dev)

    def values_out(q, n):
        got(pr.at[q], v1 + n)
        d = (q - y + 4) % 4

        @pl.when(d != 0)
        def _():
            vs[d - 1] = (pp[q, mine] + pr[q]).astype(BF16)
            pltpu.make_async_remote_copy(
                src_ref=vs.at[d - 1], dst_ref=vr.at[d - 1], send_sem=ssem.at[v2 + d - 1],
                recv_sem=rsem.at[v2 + d - 1], device_id=y_dev(d), device_id_type=MESH,
            ).start()

    values_of(x, 0)
    o_id = new_id(8)
    for p in range(2):
        got(wbuf.at[xl, lo, p], w2 + 6 * p)
        send_block(xl, lo, p, 4, xr_dev)
        got(wbuf.at[xr, hi, p], w2 + 6 * p + 1)
        send_block(xr, hi, p, 5, xl_dev)
        for n in range(3):
            got(zr.at[p, n], z_id + 3 * p + n)
        rb[p] = (
            sx[p, :, quarter_of(own_q)]
            + zr[p, 0].astype(F32) + zr[p, 1].astype(F32) + zr[p, 2].astype(F32)
        ).astype(BF16)
        for k in range(4):
            pltpu.make_async_remote_copy(
                src_ref=rb.at[p, pl.ds(16 * k, 16)], dst_ref=ob.at[z // 4, p],
                send_sem=ssem.at[o_id + 4 * p + k], recv_sem=rsem.at[o_id + 4 * p + z // 4],
                device_id=owner_dev(k), device_id_type=MESH,
            ).start()

    values_out(x, 0)
    for p in range(2):
        got(wbuf.at[xl, hi, p], w2 + 6 * p + 2)
        got(wbuf.at[xr, lo, p], w2 + 6 * p + 3)
    values_of(xl, 1)
    values_of(xr, 2)
    values_out(xl, 1)
    values_out(xr, 2)
    for p in range(2):
        got(wbuf.at[xo, lo, p], w2 + 6 * p + 4)
        got(wbuf.at[xo, hi, p], w2 + 6 * p + 5)
    values_of(xo, 3)
    values_out(xo, 3)

    for p in range(2):
        for k in range(4):
            got(ob.at[k, p], o_id + 4 * p + k)
    quarter = pl.ds(pl.multiple_of(16 * r, 16), 16)
    gf[:, quarter, :] = (
        ob[0].astype(F32) + ob[1].astype(F32) + ob[2].astype(F32) + ob[3].astype(F32)
    ) * (1.0 / RANKS)
    f_id = new_id(3)
    for d in (1, 2, 3):
        rd = (r + d) % 4
        send(gf.at[:, quarter], gf.at[:, quarter], f_id + d - 1, (y, s, rd))

    for d in (1, 2, 3):
        got(vr.at[d - 1], v2 + d - 1)
    vals[...] = (
        pp[y, mine] + pr[y] + vr[0].astype(F32) + vr[1].astype(F32) + vr[2].astype(F32)
    ).astype(BF16)

    def backward_head(h, acc):
        lanes = pl.ds(pl.multiple_of(h * HD, HD), HD)
        gw = lax.dot_general(vals[...], gov[:, lanes], NT, preferred_element_type=F32)
        weights = wst[h]
        dots = jnp.sum(weights.astype(BF16).astype(F32) * gw, axis=0, keepdims=True)
        gs = (weights * (gw - dots) * FACTOR).astype(BF16)
        gq = jnp.dot(ktr[...], gs, preferred_element_type=F32)
        gqv[:, lanes] = gq.T.astype(BF16)
        return acc + jnp.dot(gs, qv[:, lanes], preferred_element_type=F32)

    gkv[...] = lax.fori_loop(
        0, HEADS, backward_head, jnp.zeros((TOK, HD), F32), unroll=2
    ).astype(BF16)
    outs = [pltpu.make_async_copy(gqv, o_gq, lsem.at[8]), pltpu.make_async_copy(gkv, o_gk, lsem.at[9])]
    for cp in outs:
        cp.start()

    for d in (1, 2, 3):
        other = pl.ds(pl.multiple_of(16 * ((r - d + 4) % 4), 16), 16)
        got(gf.at[:, other], f_id + d - 1)
    for cp in copies[5:]:
        cp.wait()
    gradient = gf[...].reshape(HD, QTR).T
    new_first = BETA_FIRST * fstv[...] + (1.0 - BETA_FIRST) * gradient
    new_second = BETA_SECOND * sndv[...] + (1.0 - BETA_SECOND) * gradient * gradient
    corrected = (
        new_first
        / (1.0 - BETA_FIRST**STEP)
        / (jnp.sqrt(new_second / (1.0 - BETA_SECOND**STEP)) + EPSILON)
    )
    og[...] = gradient
    om[...] = masv[...] - LEARN_RATE * (corrected + WEIGHT_DECAY * masv[...])
    of[...] = new_first
    osn[...] = new_second
    for n, (a, b) in enumerate(((og, o_grad), (om, o_mas), (of, o_fst), (osn, o_snd))):
        cp = pltpu.make_async_copy(a, b, lsem.at[10 + n])
        cp.start()
        outs.append(cp)

    for src, i in sends:
        pltpu.make_async_copy(src, src, ssem.at[i]).wait()
    for d in (1, 2, 3):
        pltpu.make_async_copy(vs.at[d - 1], vs.at[d - 1], ssem.at[v2 + d - 1]).wait()
    for p in range(2):
        for k in range(4):
            src = rb.at[p, pl.ds(16 * k, 16)]
            pltpu.make_async_copy(src, src, ssem.at[o_id + 4 * p + k]).wait()
    for cp in outs:
        cp.wait()


def hand_over(*refs):
    src, dst, held, sem = refs[:6], refs[6:12], refs[12:18], refs[18]
    moves = []
    for n in range(6):
        rows = src[n].shape[0] // (4 if n == 0 else 1)
        moves += [(n, pl.ds(rows * k, rows)) for k in range(4 if n == 0 else 1)]
    into = [
        pltpu.make_async_copy(src[n].at[rows], held[n].at[rows], sem.at[0, i])
        for i, (n, rows) in enumerate(moves)
    ]
    out = [
        pltpu.make_async_copy(held[n].at[rows], dst[n].at[rows], sem.at[1, i])
        for i, (n, rows) in enumerate(moves)
    ]
    for cp in into:
        cp.start()
    for cp, after in zip(into, out):
        cp.wait()
        after.start()
    for cp in out:
        cp.wait()


N_SEM = 64


def per_device(act, que, key, gout, seg, wgt, mas, fst, snd):
    sds = jax.ShapeDtypeStruct
    any_spec = pl.BlockSpec(memory_space=pl.ANY)
    vm = pltpu.VMEM
    shard = (QTR, HD)
    results = pl.pallas_call(
        kernel,
        out_shape=(
            sds((TOK, HALF), BF16), sds((TOK, HD), BF16),
            sds(shard, F32), sds(shard, F32), sds(shard, F32), sds(shard, F32),
        ),
        in_specs=[any_spec] * 9,
        out_specs=[any_spec] * 6,
        scratch_shapes=[
            vm((2 * TOK, HALF), BF16),
            vm((TOK, HEADS * HD), BF16), vm((TOK, HD), BF16), vm((TOK, HEADS * HD), BF16),
            vm((1, TOK), jnp.int32), vm(shard, F32), vm(shard, F32), vm(shard, F32),
            vm((4, 4, 2, HD, HD), BF16),
            vm((TOK, TOK), F32),
            vm((HEADS, TOK, TOK), F32),
            vm((TOK, HD), F32),
            vm((4 * HD, 2 * TOK), BF16),
            vm((2, 6, CH, HALF // 2), BF16),
            vm((2, 2, CH, HALF // 2), F32),
            vm((2, 6, CH, HALF // 2), BF16),
            vm((2, CH, HALF), F32),
            vm((2, 6, CH, QTR), BF16),
            vm((2, CH, QTR), BF16),
            vm((4, 2, 16, QTR), BF16),
            vm((2, CH, QTR), F32),
            vm((4, 2 * TOK, HD), F32),
            vm((4, TOK, HD), F32),
            vm((3, TOK, HD), BF16),
            vm((3, TOK, HD), BF16),
            vm((TOK, HD), BF16),
            vm((HD, TOK), BF16),
            vm((TOK, HD), F32),
            vm((TOK, HEADS * HD), BF16), vm((TOK, HD), BF16),
            vm(shard, F32), vm(shard, F32), vm(shard, F32), vm(shard, F32),
            pltpu.SemaphoreType.DMA((N_SEM,)),
            pltpu.SemaphoreType.DMA((N_SEM,)),
            pltpu.SemaphoreType.DMA((16,)),
        ],
        compiler_params=pltpu.CompilerParams(
            collective_id=0, has_side_effects=True, vmem_limit_bytes=60 << 20
        ),
    )(act, que, key, gout, seg.reshape(1, TOK), wgt, mas, fst, snd)
    return pl.pallas_call(
        hand_over,
        out_shape=tuple(sds(v.shape, v.dtype) for v in results),
        in_specs=[any_spec] * 6,
        out_specs=[any_spec] * 6,
        scratch_shapes=[vm(v.shape, v.dtype) for v in results] + [pltpu.SemaphoreType.DMA((2, 9))],
        compiler_params=pltpu.CompilerParams(vmem_limit_bytes=60 << 20),
    )(*results)


def solution(mesh):
    token = P(("shard", "replica"), "tensor")
    row = P("shard", "tensor")
    return jax.shard_map(
        per_device,
        mesh=mesh,
        in_specs=(token, token, token, token, P(("shard", "replica")), row, row, row, row),
        out_specs=(token, token, row, row, row, row),
        check_vma=False,
    )
```
